512 devices in a mesh: dp: 16 (over z_hi, y), cent: 32 (over x, z_lo, core).
Axes of the slice: x: 4, y: 8, z: 8 (z_hi: 2, z_lo: 4; z = z_hi * 4 + z_lo), core: 2. Of those that a mesh axis runs over, the one named last changes fastest.
Arguments:
- vectors: bfloat16 [131072, 1024], P(('dp', 'cent')), may hold values from -6 to 6
- candidates: int32 [131072, 4], P(('dp', 'cent')), may hold values from 0 to 31, all different within a row; in each aligned block of 256 rows (0 to 255, 256 to 511, ...) at most 64 rows name the same one
- centroids: bfloat16 [8192, 1024], P('cent', 'dp'), may hold values from -6 to 6
Outputs:
- new_centroids: float32 [8192, 1024], P('cent', 'dp')
- mass: float32 [8192], P('cent')
The draws below stay inside these ranges and needn't reach their ends.
Inputs may be any that keep to these rules, and one draw needn't show every extreme that they name: `candidates`: each row names 4 different blocks. Within the 256 rows of one device (aligned blocks of rows, in order) no block is named by more than 64 rows, and some block by exactly 64. Every block is named by some row.
All inputs are finite; a program needn't handle non-finite values.
Results may differ from the reference program's by a relative error of at most 0.02.
The reference program's roundings to bfloat16 on the way count: a program that leaves them out, or rounds other values in their place, can miss the bound.
Values may be sent and summed in bfloat16 or wider, within the bound.
A program may use at most 64 MiB of HBM per device.

```python
import math
import jax
import jax.numpy as jnp
import numpy as np
from jax import lax

D = 1024
BLOCK = 256
TOP = 4
ITERS = 2
V_DEV = 256
N = 131072
K = 8192
CAP = 64
N_DP = 16
N_CENT = 32


def block_scale(rng, extent, shards, smallest, high):
    factor_of = 1.0
    for dim, blocks in shards:
        draws = jax.random.uniform(jax.random.fold_in(jax.random.fold_in(rng, 6), dim), (blocks,), jnp.float32, smallest / len(shards), high / len(shards))
        factor_of = factor_of * jnp.repeat(jnp.exp(draws), extent[dim] // blocks).reshape((-1,) + (1,) * (len(extent) - 1 - dim))
    return factor_of


def routed_block(key, own, number, rows, count, top, limit, skew):
    ranking = jax.random.permutation(key, count)
    heavy_load, ordinary = load_shares(count, rows * top, limit, skew, True), load_shares(count, rows * top, limit, skew, False)
    places = jnp.arange(count)

    def named(sizes, rotation):
        used = int((sizes > 0).sum())
        fixed = max(1, used // 4)
        passed = fixed + (places - fixed + rotation * (used - fixed)) % max(1, count - fixed)
        return jnp.zeros((count,), jnp.int32).at[ranking[jnp.where(places < fixed, places, passed)]].set(jnp.asarray(sizes, jnp.int32))

    sizes = jnp.where(number % 4 == 0, named(heavy_load, number // 4), named(ordinary, number - number // 4 - 1))
    mixed = jax.random.permutation(jax.random.fold_in(own, 3), count)
    donor, sink = mixed[0:count // 2 * 2:2], mixed[1:count // 2 * 2:2]
    slack = jnp.minimum(sizes[donor] - 1, limit - sizes[sink]) // 2
    slack = jnp.where((donor == ranking[0]) | (sink == ranking[0]) | (sizes[sink] == 0), 0, jnp.maximum(slack, 0))
    passed = jax.random.randint(jax.random.fold_in(own, 4), (count // 2,), 0, 1 << 20) % (slack + 1)
    sizes = sizes.at[donor].add(-passed).at[sink].add(passed)
    items = jnp.searchsorted(jnp.cumsum(sizes), jnp.arange(rows * top), side="right").astype(jnp.int32)
    listing = items.reshape(top, rows).T
    listing = listing[jax.random.permutation(jax.random.fold_in(own, 1), rows)]
    rotation = jax.random.randint(jax.random.fold_in(own, 2), (rows, 1), 0, top)
    return jnp.take_along_axis(listing, (jnp.arange(top)[None, :] + rotation) % top, axis=1)


def load_shares(count, total, bound, slope, full):
    loads = [(1 << 20) // math.isqrt(standing ** slope) + 1 for standing in range(1, count + 1)]
    largest = bound if full else min(bound, max(-(-total // count), total * loads[0] // sum(loads)))
    least = 1 if total - largest >= count - 1 else 0
    given, spare = [largest] + [least] * (count - 1), total - largest - least * (count - 1)
    while spare > 0:
        movable = [i for i in range(1, count) if given[i] < largest] or [i for i in range(1, count) if given[i] < bound]
        pool, remaining = sum([loads[i] for i in movable]), spare
        for i in movable:
            addition = min(bound - given[i], max(1, remaining * loads[i] // pool), spare)
            given[i] = given[i] + addition
            spare = spare - addition
    return np.array(given)


def noise(own_key, shape, spread, limit, pieces=(), kind=jnp.bfloat16):
    loudness = block_scale(own_key, shape, pieces, -0.22, 0.18) if pieces else 1.0
    values = jax.random.normal(own_key, shape, jnp.float32) * spread * loudness
    return jnp.minimum(jnp.maximum(values, -limit), limit).astype(kind)


def setup_inputs(seed: int = 0) -> dict:
    streams_of = jax.random.split(jax.random.key(seed), 4)
    vectors = noise(streams_of[0], (N, D), 1.0, 6.0, ((0, 512),))
    candidates_keys = jax.random.split(jax.random.fold_in(streams_of[1], 1), N // V_DEV)
    candidates_turns = jax.random.permutation(jax.random.fold_in(streams_of[1], 3), N // V_DEV)
    candidates = jax.vmap(lambda own, number: routed_block(jax.random.fold_in(streams_of[1], 2), own, number, V_DEV, N_CENT, TOP, CAP, 2))(candidates_keys, candidates_turns).reshape((N, TOP))
    centroids = noise(streams_of[2], (K, D), 1.0, 6.0, ((0, 32), (1, 16)))
    return {"vectors": vectors, "candidates": candidates, "centroids": centroids}


EPSILON = 1e-06
SHARPNESS = 20.0

def rms_unit(matrix):
    return matrix * lax.rsqrt(lax.optimization_barrier(jnp.mean(matrix * matrix, axis=-1, keepdims=True)) + EPSILON)

def reference(vectors, candidates, centroids):
    vec_count = vectors.shape[0]
    unit_vec = rms_unit(vectors.astype(jnp.float32)).astype(jnp.bfloat16)
    padded = jnp.concatenate([unit_vec.astype(jnp.float32), jnp.zeros((1, D), jnp.float32)], axis=0)
    slots = CAP * N_DP * N_CENT
    blocks = K // BLOCK
    block_ids = jnp.arange(blocks, dtype=jnp.int32)

    def members(block):
        wanted = jnp.any(candidates == block, axis=1)
        return jnp.nonzero(wanted, size=slots, fill_value=vec_count)[0].astype(jnp.int32)
    member_table = lax.map(members, block_ids)
    current = centroids
    new_centroids = None
    mass = None
    for sweep in range(ITERS):
        unit_cent = rms_unit(current.astype(jnp.float32)).astype(jnp.bfloat16)
        unit_cent = unit_cent.astype(jnp.float32).reshape(blocks, BLOCK, D)

        def raw_of(block):
            chosen = jnp.take(padded, member_table[block], axis=0)
            scores = jnp.dot(chosen, unit_cent[block].T, precision=lax.Precision.HIGHEST, preferred_element_type=jnp.float32)
            return jnp.exp(scores * (SHARPNESS / D))

        def add_total(totals, block):
            raw = raw_of(block)
            return (totals.at[member_table[block]].add(lax.optimization_barrier(jnp.sum(raw, axis=1))), None)
        totals, _ = lax.scan(add_total, jnp.zeros((vec_count + 1,), jnp.float32), block_ids)

        def sum_block(block):
            members_here = member_table[block]
            raw = raw_of(block)
            live_rows = (members_here < vec_count)[:, None]
            shares = jnp.where(live_rows, raw / jnp.take(totals, members_here)[:, None], 0.0)
            chosen = jnp.take(padded, members_here, axis=0)
            shares_low = shares.astype(jnp.bfloat16).astype(jnp.float32)
            block_sums = jnp.dot(shares_low.T, chosen, precision=lax.Precision.HIGHEST, preferred_element_type=jnp.float32)
            return (block_sums, lax.optimization_barrier(jnp.sum(shares, axis=0)))
        sums, masses = lax.map(sum_block, block_ids)
        new_centroids = rms_unit(sums.reshape(K, D))
        mass = masses.reshape(K)
        current = new_centroids.astype(jnp.bfloat16)
    return (new_centroids, mass)
```

```python
import functools

import jax
import jax.numpy as jnp
from jax import lax
from jax.experimental import pallas as pl
from jax.experimental.pallas import tpu as pltpu
from jax.sharding import PartitionSpec as P

ITERS = 2
EPSILON = 1e-06
SHARPNESS = 20.0

D = 1024
ROWS = 256
BLOCK = 256
CAP = 64
N_DP = 16
N_CENT = 32
N_X = 4
N_Z = 4
LAYER = 8
SLOTS = N_CENT * CAP
PANEL = D // N_DP

F32 = jnp.float32
BF16 = jnp.bfloat16
MESH = pl.DeviceIdType.MESH


def cent_of(place):
    return ((place // 2) % N_X) * LAYER + (place // LAYER) * 2 + place % 2


def lanes(start, size):
    return pl.ds(pl.multiple_of(start, 128), size)


def kernel(
    vec_ref,
    cand_ref,
    cent_ref,
    out_ref,
    mass_ref,
    units,
    ranks,
    own_pick,
    packed,
    rows,
    raw,
    low,
    part,
    part_in,
    total,
    total_in,
    wide,
    unit_cent,
    panel_out,
    panel_in,
    fresh,
    edge_out,
    edge_in,
    z_send,
    z_recv,
    rank_send,
    rank_recv,
    x_send,
    x_recv,
    part_send,
    part_recv,
    total_send,
    total_recv,
    panel_send,
    panel_recv,
    fresh_send,
    fresh_recv,
    edge_send,
    edge_recv,
):
    dp = lax.axis_index("dp")
    cent = lax.axis_index("cent")
    x = cent // LAYER
    z = (cent // 2) % N_Z
    core = cent % 2
    here = z * LAYER + x * 2 + core

    def dp_peer(i):
        return lax.rem(dp + i, N_DP)

    def place_peer(i):
        return lax.rem(here + i, N_CENT)

    barrier = pltpu.get_barrier_semaphore()

    def greet_cent(i, carry):
        pl.semaphore_signal(
            barrier, inc=1, device_id=(dp, cent_of(place_peer(i))), device_id_type=MESH
        )
        return carry

    def greet_dp(i, carry):
        pl.semaphore_signal(barrier, inc=1, device_id=(dp_peer(i), cent), device_id_type=MESH)
        return carry

    lax.fori_loop(1, N_CENT, greet_cent, 0)
    lax.fori_loop(1, N_DP, greet_dp, 0)

    vec = vec_ref[...].astype(F32)
    vec_scale = lax.rsqrt(jnp.mean(vec * vec, axis=1, keepdims=True) + EPSILON)
    units[z] = (vec * vec_scale).astype(BF16)
    cand = cand_ref[...]
    place = lax.broadcasted_iota(jnp.int32, (N_CENT, ROWS), 0)
    block = ((place >> 1) & (N_X - 1)) * LAYER + (place >> 3) * 2 + (place & 1)
    named = cand[0:1, :] == block
    for j in range(1, cand.shape[0]):
        named = jnp.logical_or(named, cand[j : j + 1, :] == block)
    named_f = jnp.where(named, 1.0, 0.0)
    first = lax.broadcasted_iota(jnp.int32, (ROWS, ROWS), 0)
    second = lax.broadcasted_iota(jnp.int32, (ROWS, ROWS), 1)
    before = jnp.where(first < second, 1.0, 0.0).astype(BF16)
    rank = jnp.dot(named_f.astype(BF16), before, preferred_element_type=F32)
    slots = jnp.where(named, rank, -1.0).astype(jnp.int32)
    for layer in range(N_Z):
        ranks[layer, 0] = slots[layer * LAYER : (layer + 1) * LAYER]

    slot_iota = lax.broadcasted_iota(jnp.int32, (CAP, ROWS), 0)

    def pick_rows(rank_rows):
        picks = [
            jnp.where(rank_rows[j : j + 1, :] == slot_iota, 1.0, 0.0).astype(BF16)
            for j in range(LAYER)
        ]
        return jnp.concatenate(picks, axis=0)

    panel0 = cent_ref[...]
    half = BLOCK // 2
    fresh[0, dp] = jnp.concatenate([panel0[:half], panel0[half:]], axis=1)

    pl.semaphore_wait(barrier, N_CENT - 1 + N_DP - 1)

    def rank_copy(layer):
        return pltpu.make_async_remote_copy(
            src_ref=ranks.at[layer, 0],
            dst_ref=ranks.at[z, 1],
            send_sem=rank_send.at[layer],
            recv_sem=rank_recv.at[z],
            device_id=(dp, x * LAYER + layer * 2 + core),
            device_id_type=MESH,
        )

    def unit_copy(origin, side):
        return pltpu.make_async_remote_copy(
            src_ref=units.at[origin],
            dst_ref=units.at[origin],
            send_sem=z_send.at[origin, side],
            recv_sem=z_recv.at[origin],
            device_id=(dp, x * LAYER + (z + 2 * side - 1) * 2 + core),
            device_id_type=MESH,
        )

    def start_up(origin):
        @pl.when(z < N_Z - 1)
        def _():
            unit_copy(origin, 1).start()

    def start_down(origin):
        @pl.when(z > 0)
        def _():
            unit_copy(origin, 0).start()

    start_up(z)
    start_down(z)

    def send_rank(i, carry):
        rank_copy(lax.rem(z + i, N_Z)).start()
        return carry

    lax.fori_loop(1, N_Z, send_rank, 0)

    def fresh_copy(sweep, i):
        return pltpu.make_async_remote_copy(
            src_ref=fresh.at[sweep, dp],
            dst_ref=fresh.at[sweep, dp],
            send_sem=fresh_send.at[sweep],
            recv_sem=fresh_recv.at[sweep],
            device_id=(dp_peer(i), cent),
            device_id_type=MESH,
        )

    def send_fresh(sweep):
        def step(i, carry):
            fresh_copy(sweep, i).start()
            return carry

        lax.fori_loop(1, N_DP, step, 0)

    send_fresh(0)

    def row_copy(origin, i):
        target = lax.rem(x * 2 + core + i, LAYER)
        return pltpu.make_async_remote_copy(
            src_ref=packed.at[origin, target],
            dst_ref=rows.at[origin * LAYER + x * 2 + core],
            send_sem=x_send.at[origin, target],
            recv_sem=x_recv.at[origin * LAYER + x * 2 + core],
            device_id=(dp, (target // 2) * LAYER + z * 2 + target % 2),
            device_id_type=MESH,
        )

    def pack_and_send(origin, rank_rows):
        chosen = jnp.dot(pick_rows(rank_rows), units[origin], preferred_element_type=F32)
        packed[origin] = chosen.astype(BF16).reshape(LAYER, CAP, D)
        rows[origin * LAYER + x * 2 + core] = packed[origin, x * 2 + core]

        def step(i, carry):
            row_copy(origin, i).start()
            return carry

        lax.fori_loop(1, LAYER, step, 0)

    pack_and_send(z, ranks[z, 0])

    for layer in range(N_Z):
        own_pick[layer * LAYER * CAP : (layer + 1) * LAYER * CAP] = pick_rows(ranks[layer, 0])

    def event(e, carry):
        distance = (e + 1) // 2
        up = lax.rem(e, 2)
        origin = z + jnp.where(up == 1, -distance, distance)

        @pl.when(jnp.logical_and(origin >= 0, origin < N_Z))
        def _():
            unit_copy(origin, 0).wait_recv()

            @pl.when(up == 1)
            def _():
                start_up(origin)

            @pl.when(up == 0)
            def _():
                start_down(origin)

            rank_copy_in(origin).wait_recv()
            pack_and_send(origin, ranks[origin, 1])

        return carry

    def rank_copy_in(origin):
        return pltpu.make_async_remote_copy(
            src_ref=ranks.at[origin, 0],
            dst_ref=ranks.at[origin, 1],
            send_sem=rank_send.at[origin],
            recv_sem=rank_recv.at[origin],
            device_id=(dp, x * LAYER + origin * 2 + core),
            device_id_type=MESH,
        )

    lax.fori_loop(1, 2 * N_Z - 1, event, 0)

    left = lax.broadcasted_iota(jnp.int32, (half, 128), 1) < PANEL
    left_row = lax.broadcasted_iota(jnp.int32, (1, 128), 1) < PANEL

    def take_halves(ref, sweep):
        pieces = []
        for j in range(N_CENT // 2):
            even = ref[sweep, :, 256 * j : 256 * j + 128]
            odd = ref[sweep, :, 256 * j + 128 : 256 * j + 256]
            first_core = jnp.where(left_row, even, pltpu.roll(odd, 64, 1))
            second_core = jnp.where(left_row, pltpu.roll(even, 64, 1), odd)
            pieces.append(jnp.where(core == 0, first_core, second_core))
        return jnp.concatenate(pieces, axis=1)

    def split(row):
        high = row.astype(BF16).astype(F32)
        rest = row - high
        middle = rest.astype(BF16).astype(F32)
        last = rest - middle
        zeros = jnp.zeros((5, row.shape[1]), F32)
        return jnp.concatenate([high, middle, last, zeros], axis=0).astype(BF16)

    def pair_copy(source, target, sweep, i, send_sem, recv_sem):
        other = place_peer(i)
        return pltpu.make_async_remote_copy(
            src_ref=source.at[sweep, :, lanes((other // 2) * 128, 128)],
            dst_ref=target.at[sweep, :, lanes(here * 128, 128)],
            send_sem=send_sem.at[sweep],
            recv_sem=recv_sem.at[sweep],
            device_id=(dp, cent_of(other)),
            device_id_type=MESH,
        )

    def exchange_pairs(source, target, sweep, send_sem, recv_sem):
        def step(i, carry):
            pair_copy(source, target, sweep, i, send_sem, recv_sem).start()
            return carry

        lax.fori_loop(1, N_CENT, step, 0)
        target[sweep, :, lanes(here * 128, 128)] = source[sweep, :, lanes((here // 2) * 128, 128)]
        seen = target.at[sweep, :, pl.ds(0, (N_CENT - 1) * 128)]
        pltpu.make_async_copy(seen, seen, recv_sem.at[sweep]).wait()

    def edge_copy(sweep, i):
        return pltpu.make_async_remote_copy(
            src_ref=edge_out.at[sweep],
            dst_ref=edge_in.at[sweep, dp],
            send_sem=edge_send.at[sweep],
            recv_sem=edge_recv.at[sweep],
            device_id=(dp_peer(i), cent),
            device_id_type=MESH,
        )

    def panel_copy(sweep, target):
        return pltpu.make_async_remote_copy(
            src_ref=panel_out.at[sweep, target],
            dst_ref=panel_in.at[sweep, dp],
            send_sem=panel_send.at[sweep],
            recv_sem=panel_recv.at[sweep],
            device_id=(target, cent),
            device_id_type=MESH,
        )

    def sweep_step(sweep, carry):
        seen = fresh.at[sweep, pl.ds(0, N_DP - 1)]
        pltpu.make_async_copy(seen, seen, fresh_recv.at[sweep]).wait()
        top_squares = jnp.zeros((half, 128), F32)
        bottom_squares = jnp.zeros((half, 128), F32)
        for j in range(N_DP // 2):
            even = fresh[sweep, 2 * j].astype(F32)
            odd = fresh[sweep, 2 * j + 1].astype(F32)
            top = jnp.where(left, even, pltpu.roll(odd, 64, 1))
            bottom = jnp.where(left, pltpu.roll(even, 64, 1), odd)
            wide[:half, 128 * j : 128 * (j + 1)] = top
            wide[half:, 128 * j : 128 * (j + 1)] = bottom
            top_squares += top * top
            bottom_squares += bottom * bottom
        top_scale = lax.rsqrt(jnp.sum(top_squares, axis=1, keepdims=True) / D + EPSILON)
        bottom_scale = lax.rsqrt(jnp.sum(bottom_squares, axis=1, keepdims=True) / D + EPSILON)
        unit_cent[:half] = (wide[:half] * top_scale).astype(BF16)
        unit_cent[half:] = (wide[half:] * bottom_scale).astype(BF16)

        def score(g, inner):
            distance = (g + 1) // 2
            origin = z + jnp.where(lax.rem(g, 2) == 1, -distance, distance)

            @pl.when(jnp.logical_and(origin >= 0, origin < N_Z))
            def _():
                @pl.when(sweep == 0)
                def _():
                    def arrive(i, deep):
                        sender = lax.rem(x * 2 + core + i, LAYER)
                        slot = rows.at[origin * LAYER + sender]
                        pltpu.make_async_copy(
                            slot, slot, x_recv.at[origin * LAYER + sender]
                        ).wait()
                        return deep

                    lax.fori_loop(1, LAYER, arrive, 0)

                mine = rows[pl.ds(origin * LAYER, LAYER)].reshape(LAYER * CAP, D)
                scores = lax.dot_general(
                    unit_cent[...], mine, (((1,), (1,)), ((), ())), preferred_element_type=F32
                )
                weights = jnp.exp(scores * (SHARPNESS / D))
                raw[:, lanes(origin * LAYER * CAP, LAYER * CAP)] = weights
                part[sweep, :, lanes(origin * LAYER * CAP, LAYER * CAP)] = jnp.sum(
                    weights, axis=0, keepdims=True
                )

            return inner

        lax.fori_loop(0, 2 * N_Z - 1, score, 0)

        exchange_pairs(part, part_in, sweep, part_send, part_recv)
        parts = split(take_halves(part_in, sweep))
        sums_row = jnp.sum(
            jnp.dot(parts, own_pick[...], preferred_element_type=F32), axis=0, keepdims=True
        )
        total[sweep] = jnp.sum(
            lax.dot_general(
                split(sums_row),
                own_pick[...],
                (((1,), (1,)), ((), ())),
                preferred_element_type=F32,
            ),
            axis=0,
            keepdims=True,
        )
        exchange_pairs(total, total_in, sweep, total_send, total_recv)
        totals = take_halves(total_in, sweep)
        live = totals > 0.0
        inverse = jnp.where(live, 1.0 / jnp.where(live, totals, 1.0), 0.0)

        mass_part = jnp.zeros((BLOCK, 128), F32)
        for j in range(SLOTS // 128):
            piece = slice(128 * j, 128 * (j + 1))
            shares = raw[:, piece] * inverse[:, piece]
            low[:, piece] = shares.astype(BF16)
            mass_part += shares
        mass_row = jnp.sum(jnp.transpose(mass_part), axis=0, keepdims=True)
        edge_out[sweep, 2:3, :] = mass_row[:, :128]
        edge_out[sweep, 3:4, :] = mass_row[:, 128:]

        def sum_step(j, inner):
            block_rows = rows[:, :, lanes(j * 256, 256)].reshape(SLOTS, 256)
            sums = jnp.dot(low[...], block_rows, preferred_element_type=F32)
            for k in range(2):
                top = sums[:half, 128 * k : 128 * (k + 1)]
                bottom = sums[half:, 128 * k : 128 * (k + 1)]
                even = jnp.where(left, top, pltpu.roll(bottom, 64, 1))
                odd = jnp.where(left, pltpu.roll(top, 64, 1), bottom)
                panel_out[sweep, 4 * j + 2 * k] = even.astype(BF16)
                panel_out[sweep, 4 * j + 2 * k + 1] = odd.astype(BF16)
            for k in range(4):
                target = 4 * j + k

                @pl.when(target != dp)
                def _():
                    panel_copy(sweep, target).start()

            return inner

        lax.fori_loop(0, N_DP // 4, sum_step, 0)
        panel_in[sweep, dp] = panel_out[sweep, dp]
        seen = panel_in.at[sweep, pl.ds(0, N_DP - 1)]
        pltpu.make_async_copy(seen, seen, panel_recv.at[sweep]).wait()
        sums_panel = panel_in[sweep, 0].astype(F32)
        for j in range(1, N_DP):
            sums_panel += panel_in[sweep, j].astype(F32)

        squares = jnp.transpose(sums_panel * sums_panel)
        edge_out[sweep, 0:1, :] = jnp.sum(squares[:PANEL], axis=0, keepdims=True)
        edge_out[sweep, 1:2, :] = jnp.sum(squares[PANEL:], axis=0, keepdims=True)
        edge_out[sweep, 4:8, :] = jnp.zeros((4, 128), F32)

        def send_edge(i, inner):
            edge_copy(sweep, i).start()
            return inner

        lax.fori_loop(1, N_DP, send_edge, 0)
        edge_in[sweep, dp] = edge_out[sweep]
        seen = edge_in.at[sweep, pl.ds(0, N_DP - 1)]
        pltpu.make_async_copy(seen, seen, edge_recv.at[sweep]).wait()
        edges = edge_in[sweep, 0]
        for j in range(1, N_DP):
            edges += edge_in[sweep, j]
        scales = lax.rsqrt(edges / D + EPSILON)
        scale_t = jnp.concatenate(
            [
                jnp.broadcast_to(scales[0:1], (PANEL, 128)),
                jnp.broadcast_to(scales[1:2], (PANEL, 128)),
            ],
            axis=0,
        )
        new_panel = sums_panel * jnp.transpose(scale_t)

        @pl.when(sweep < ITERS - 1)
        def _():
            fresh[sweep + 1, dp] = new_panel.astype(BF16)
            send_fresh(sweep + 1)

        @pl.when(sweep == ITERS - 1)
        def _():
            out_ref[:half] = new_panel[:, :PANEL]
            out_ref[half:] = new_panel[:, PANEL:]
            mass_ref[:, :128] = edges[2:3]
            mass_ref[:, 128:] = edges[3:4]

        return carry

    lax.fori_loop(0, ITERS, sweep_step, 0)

    def leave(sweep, carry):
        for ref, sem in ((part_in, part_send), (total_in, total_send)):
            sent = ref.at[sweep, :, pl.ds(0, (N_CENT - 1) * 128)]
            pltpu.make_async_copy(sent, sent, sem.at[sweep]).wait()
        for ref, sem in ((panel_in, panel_send), (edge_in, edge_send), (fresh, fresh_send)):
            sent = ref.at[sweep, pl.ds(0, N_DP - 1)]
            pltpu.make_async_copy(sent, sent, sem.at[sweep]).wait()
        return carry

    lax.fori_loop(0, ITERS, leave, 0)

    def leave_origin(origin, carry):
        def step(i, inner):
            row_copy(origin, i).wait_send()
            return inner

        lax.fori_loop(1, LAYER, step, 0)

        @pl.when(jnp.logical_and(origin <= z, z < N_Z - 1))
        def _():
            unit_copy(origin, 1).wait_send()

        @pl.when(jnp.logical_and(origin >= z, z > 0))
        def _():
            unit_copy(origin, 0).wait_send()

        @pl.when(origin != z)
        def _():
            rank_copy(origin).wait_send()

        return carry

    lax.fori_loop(0, N_Z, leave_origin, 0)


def body(vectors, candidates, centroids):
    vmem = pl.BlockSpec(memory_space=pltpu.VMEM)
    dma = pltpu.SemaphoreType.DMA
    panel, mass = pl.pallas_call(
        kernel,
        out_shape=(
            jax.ShapeDtypeStruct((BLOCK, PANEL), F32),
            jax.ShapeDtypeStruct((1, BLOCK), F32),
        ),
        in_specs=[vmem] * 3,
        out_specs=(vmem, vmem),
        scratch_shapes=[
            pltpu.VMEM((N_Z, ROWS, D), BF16),
            pltpu.VMEM((N_Z, 2, LAYER, ROWS), jnp.int32),
            pltpu.VMEM((SLOTS, ROWS), BF16),
            pltpu.VMEM((N_Z, LAYER, CAP, D), BF16),
            pltpu.VMEM((N_CENT, CAP, D), BF16),
            pltpu.VMEM((BLOCK, SLOTS), F32),
            pltpu.VMEM((BLOCK, SLOTS), BF16),
            pltpu.VMEM((ITERS, 1, SLOTS), F32),
            pltpu.VMEM((ITERS, 1, N_CENT * 128), F32),
            pltpu.VMEM((ITERS, 1, SLOTS), F32),
            pltpu.VMEM((ITERS, 1, N_CENT * 128), F32),
            pltpu.VMEM((BLOCK, D), F32),
            pltpu.VMEM((BLOCK, D), BF16),
            pltpu.VMEM((ITERS, N_DP, 128, 128), BF16),
            pltpu.VMEM((ITERS, N_DP, 128, 128), BF16),
            pltpu.VMEM((ITERS, N_DP, 128, 128), BF16),
            pltpu.VMEM((ITERS, 8, 128), F32),
            pltpu.VMEM((ITERS, N_DP, 8, 128), F32),
            dma((N_Z, 2)),
            dma((N_Z,)),
            dma((N_Z,)),
            dma((N_Z,)),
            dma((N_Z, LAYER)),
            dma((N_CENT,)),
            dma((ITERS,)),
            dma((ITERS,)),
            dma((ITERS,)),
            dma((ITERS,)),
            dma((ITERS,)),
            dma((ITERS,)),
            dma((ITERS,)),
            dma((ITERS,)),
            dma((ITERS,)),
            dma((ITERS,)),
        ],
        compiler_params=pltpu.CompilerParams(
            collective_id=0, has_side_effects=True, vmem_limit_bytes=48 * 1024 * 1024
        ),
        cost_estimate=pl.CostEstimate(
            flops=9 * 2 * SLOTS * BLOCK * D // 2, bytes_accessed=4 << 20, transcendentals=SLOTS * BLOCK
        ),
        name="soft_kmeans",
    )(vectors, candidates.T, centroids)
    return panel, mass.reshape(BLOCK)


def solution(mesh):
    return jax.shard_map(
        body,
        mesh=mesh,
        in_specs=(P(("dp", "cent"), None), P(("dp", "cent"), None), P("cent", "dp")),
        out_specs=(P("cent", "dp"), P("cent")),
        check_vma=False,
    )
```

```python
import functools

import jax
import jax.numpy as jnp
from jax import lax
from jax.experimental import pallas as pl
from jax.experimental.pallas import tpu as pltpu
from jax.sharding import PartitionSpec as P

ITERS = 2
EPSILON = 1e-06
SHARPNESS = 20.0

D = 1024
ROWS = 256
BLOCK = 256
CAP = 64
N_DP = 16
N_CENT = 32
N_X = 4
N_Y = 8
N_Z = 4
LAYER = 8
SLOTS = N_CENT * CAP
PANEL = D // N_DP

F32 = jnp.float32
BF16 = jnp.bfloat16
MESH = pl.DeviceIdType.MESH


def lanes(start, size):
    return pl.ds(pl.multiple_of(start, 128), size)


def kernel(
    vec_ref,
    cand_ref,
    cent_ref,
    out_ref,
    mass_ref,
    units,
    ranks,
    picks,
    packed,
    rows,
    raw,
    low,
    part,
    part_in,
    line_in,
    total,
    total_in,
    wide,
    unit_cent,
    panel_out,
    panel_in,
    fresh,
    edge_out,
    edge_in,
    z_send,
    z_recv,
    rank_send,
    rank_recv,
    x_send,
    x_recv,
    pair_sems,
    first_sems,
    part_send,
    part_recv,
    line_send,
    line_recv,
    total_send,
    total_recv,
    panel_send,
    panel_recv,
    fresh_send,
    fresh_recv,
    edge_send,
    edge_recv,
):
    dp = lax.axis_index("dp")
    cent = lax.axis_index("cent")
    x = cent // LAYER
    z = (cent // 2) % N_Z
    core = cent % 2
    seat = x * 2 + core

    def dp_peer(i):
        return lax.rem(dp + i, N_DP)

    def seat_peer(i):
        return lax.rem(seat + i, LAYER)

    def z_peer(i):
        return lax.rem(z + i, N_Z)

    def at_seat(other):
        return (dp, (other // 2) * LAYER + z * 2 + other % 2)

    def at_layer(other):
        return (dp, x * LAYER + other * 2 + core)

    barrier = pltpu.get_barrier_semaphore()

    def greet_seat(i, carry):
        pl.semaphore_signal(barrier, inc=1, device_id=at_seat(seat_peer(i)), device_id_type=MESH)
        return carry

    def greet_layer(i, carry):
        pl.semaphore_signal(barrier, inc=1, device_id=at_layer(z_peer(i)), device_id_type=MESH)
        return carry

    def greet_dp(i, carry):
        pl.semaphore_signal(barrier, inc=1, device_id=(dp_peer(i), cent), device_id_type=MESH)
        return carry

    lax.fori_loop(1, LAYER, greet_seat, 0)
    lax.fori_loop(1, N_Z, greet_layer, 0)
    lax.fori_loop(1, N_DP, greet_dp, 0)

    vec = vec_ref[...].astype(F32)
    vec_scale = lax.rsqrt(jnp.mean(vec * vec, axis=1, keepdims=True) + EPSILON)
    units[z] = (vec * vec_scale).astype(BF16)
    cand = cand_ref[...]
    place = lax.broadcasted_iota(jnp.int32, (N_CENT, ROWS), 0)
    block = ((place >> 1) & (N_X - 1)) * LAYER + (place >> 3) * 2 + (place & 1)
    named = cand[0:1, :] == block
    for j in range(1, cand.shape[0]):
        named = jnp.logical_or(named, cand[j : j + 1, :] == block)
    named_f = jnp.where(named, 1.0, 0.0)
    first = lax.broadcasted_iota(jnp.int32, (ROWS, ROWS), 0)
    second = lax.broadcasted_iota(jnp.int32, (ROWS, ROWS), 1)
    before = jnp.where(first < second, 1.0, 0.0).astype(BF16)
    rank = jnp.dot(named_f.astype(BF16), before, preferred_element_type=F32)
    slots = jnp.where(named, rank, -1.0).astype(jnp.int32)
    for layer in range(N_Z):
        ranks[layer, 0] = slots[layer * LAYER : (layer + 1) * LAYER]

    slot_iota = lax.broadcasted_iota(jnp.int32, (CAP, ROWS), 0)

    def pick_rows(rank_rows):
        picks = [
            jnp.where(rank_rows[j : j + 1, :] == slot_iota, 1.0, 0.0).astype(BF16)
            for j in range(LAYER)
        ]
        return jnp.concatenate(picks, axis=0)

    panel0 = cent_ref[...]
    half = BLOCK // 2
    quarter = half // 2
    for h in range(2):
        fresh[0, h, dp] = jnp.concatenate(
            [panel0[half * h : half * h + quarter], panel0[half * h + quarter : half * (h + 1)]],
            axis=1,
        )

    pl.semaphore_wait(barrier, LAYER - 1 + N_Z - 1 + N_DP - 1)

    def rank_copy(layer):
        return pltpu.make_async_remote_copy(
            src_ref=ranks.at[layer, 0],
            dst_ref=ranks.at[z, 1],
            send_sem=rank_send.at[layer],
            recv_sem=rank_recv.at[z],
            device_id=at_layer(layer),
            device_id_type=MESH,
        )

    def unit_copy(origin, side):
        return pltpu.make_async_remote_copy(
            src_ref=units.at[origin],
            dst_ref=units.at[origin],
            send_sem=z_send.at[origin, side],
            recv_sem=z_recv.at[origin],
            device_id=at_layer(z + 2 * side - 1),
            device_id_type=MESH,
        )

    def start_up(origin):
        @pl.when(z < N_Z - 1)
        def _():
            unit_copy(origin, 1).start()

    def start_down(origin):
        @pl.when(z > 0)
        def _():
            unit_copy(origin, 0).start()

    start_up(z)
    start_down(z)

    def send_rank(i, carry):
        rank_copy(z_peer(i)).start()
        return carry

    lax.fori_loop(1, N_Z, send_rank, 0)

    other_dp = lax.rem(dp + N_DP // 2, N_DP)
    pair_copy = pltpu.make_async_remote_copy(
        src_ref=fresh.at[0, :, dp],
        dst_ref=fresh.at[0, :, dp],
        send_sem=pair_sems.at[0],
        recv_sem=pair_sems.at[1],
        device_id=(other_dp, cent),
        device_id_type=MESH,
    )
    pair_copy.start()

    def first_copy(which, i):
        y_peer = (dp // N_Y) * N_Y + lax.rem(dp + i, N_Y)
        return pltpu.make_async_remote_copy(
            src_ref=fresh.at[0, :, which],
            dst_ref=fresh.at[0, :, which],
            send_sem=first_sems.at[0],
            recv_sem=first_sems.at[1],
            device_id=(y_peer, cent),
            device_id_type=MESH,
        )

    def fresh_copy(sweep, h, i):
        return pltpu.make_async_remote_copy(
            src_ref=fresh.at[sweep, h, dp],
            dst_ref=fresh.at[sweep, h, dp],
            send_sem=fresh_send.at[h],
            recv_sem=fresh_recv.at[h],
            device_id=(dp_peer(i), cent),
            device_id_type=MESH,
        )

    def row_copy(origin, i):
        target = seat_peer(i)
        return pltpu.make_async_remote_copy(
            src_ref=packed.at[origin, target],
            dst_ref=rows.at[origin * LAYER + seat],
            send_sem=x_send.at[origin, target],
            recv_sem=x_recv.at[origin * LAYER + seat],
            device_id=at_seat(target),
            device_id_type=MESH,
        )

    def pack_and_send(origin, rank_rows):
        picks[origin] = pick_rows(rank_rows)
        chosen = jnp.dot(picks[origin], units[origin], preferred_element_type=F32)
        packed[origin] = chosen.astype(BF16).reshape(LAYER, CAP, D)
        rows[origin * LAYER + seat] = packed[origin, seat]

        def step(i, carry):
            row_copy(origin, i).start()
            return carry

        lax.fori_loop(1, LAYER, step, 0)

    pack_and_send(z, ranks[z, 0])

    pair_copy.wait_recv()

    def send_first(i, carry):
        first_copy(dp, i).start()
        first_copy(other_dp, i).start()
        return carry

    lax.fori_loop(1, N_Y, send_first, 0)

    def event(e, carry):
        distance = (e + 1) // 2
        up = lax.rem(e, 2)
        origin = z + jnp.where(up == 1, -distance, distance)

        @pl.when(jnp.logical_and(origin >= 0, origin < N_Z))
        def _():
            unit_copy(origin, 0).wait_recv()

            @pl.when(up == 1)
            def _():
                start_up(origin)

            @pl.when(up == 0)
            def _():
                start_down(origin)

            rank_copy_in(origin).wait_recv()
            pack_and_send(origin, ranks[origin, 1])

        return carry

    def rank_copy_in(origin):
        return pltpu.make_async_remote_copy(
            src_ref=ranks.at[origin, 0],
            dst_ref=ranks.at[origin, 1],
            send_sem=rank_send.at[origin],
            recv_sem=rank_recv.at[origin],
            device_id=at_layer(origin),
            device_id_type=MESH,
        )

    lax.fori_loop(1, 2 * N_Z - 1, event, 0)

    left = lax.broadcasted_iota(jnp.int32, (quarter, 128), 1) < PANEL
    left_four = lax.broadcasted_iota(jnp.int32, (N_Z, 128), 1) < CAP
    left_row = lax.broadcasted_iota(jnp.int32, (1, 128), 1) < PANEL
    layer_iota = lax.broadcasted_iota(jnp.int32, (LAYER, 1), 0)

    def take_halves(ref, sweep):
        pieces = []
        for j in range(LAYER // 2):
            even = ref[sweep, 2 * j]
            odd = ref[sweep, 2 * j + 1]
            first_core = jnp.where(left_four, even, pltpu.roll(odd, 64, 1))
            second_core = jnp.where(left_four, pltpu.roll(even, 64, 1), odd)
            pieces.append(jnp.where(core == 0, first_core, second_core))
        return jnp.concatenate(pieces, axis=1)

    def split(four):
        zeros = jnp.zeros((LAYER - N_Z, four.shape[1]), F32)
        value = jnp.concatenate([four, zeros], axis=0)
        high = value.astype(BF16).astype(F32)
        rest = value - high
        middle = rest.astype(BF16).astype(F32)
        return jnp.concatenate([high, middle, rest - middle], axis=0).astype(BF16)

    def own_row(product, layer):
        added = product[:LAYER] + product[LAYER : 2 * LAYER] + product[2 * LAYER :]
        return jnp.where(layer_iota == layer, added, 0.0)

    def seat_copy(source, target, sweep, i, send_sem, recv_sem):
        other = seat_peer(i)
        return pltpu.make_async_remote_copy(
            src_ref=source.at[sweep, other // 2],
            dst_ref=target.at[sweep, seat],
            send_sem=send_sem.at[sweep],
            recv_sem=recv_sem.at[sweep],
            device_id=at_seat(other),
            device_id_type=MESH,
        )

    def exchange_seats(source, target, sweep, send_sem, recv_sem):
        def step(i, carry):
            seat_copy(source, target, sweep, i, send_sem, recv_sem).start()
            return carry

        lax.fori_loop(1, LAYER, step, 0)
        target[sweep, seat] = source[sweep, x]
        seen = target.at[sweep, pl.ds(0, LAYER - 1)]
        pltpu.make_async_copy(seen, seen, recv_sem.at[sweep]).wait()

    def line_copy(sweep, i):
        return pltpu.make_async_remote_copy(
            src_ref=line_in.at[sweep, z],
            dst_ref=line_in.at[sweep, z],
            send_sem=line_send.at[sweep],
            recv_sem=line_recv.at[sweep],
            device_id=at_layer(z_peer(i)),
            device_id_type=MESH,
        )

    def edge_copy(sweep, h, i):
        return pltpu.make_async_remote_copy(
            src_ref=edge_out.at[sweep, h],
            dst_ref=edge_in.at[sweep, h, dp],
            send_sem=edge_send.at[sweep, h],
            recv_sem=edge_recv.at[sweep, h],
            device_id=(dp_peer(i), cent),
            device_id_type=MESH,
        )

    def panel_copy(sweep, h, target):
        return pltpu.make_async_remote_copy(
            src_ref=panel_out.at[sweep, h, target],
            dst_ref=panel_in.at[sweep, h, dp],
            send_sem=panel_send.at[sweep, h],
            recv_sem=panel_recv.at[sweep, h],
            device_id=(target, cent),
            device_id_type=MESH,
        )

    def sweep_step(sweep, carry):
        @pl.when(sweep == 0)
        def _():
            seen = fresh.at[0, :, pl.ds(0, 2 * (N_Y - 1))]
            pltpu.make_async_copy(seen, seen, first_sems.at[1]).wait()

        for h in range(2):
            @pl.when(sweep > 0)
            def _():
                seen = fresh.at[sweep, h, pl.ds(0, N_DP - 1)]
                pltpu.make_async_copy(seen, seen, fresh_recv.at[h]).wait()

            low_row, high_row = half * h, half * h + quarter
            top_squares = jnp.zeros((quarter, 128), F32)
            bottom_squares = jnp.zeros((quarter, 128), F32)
            for j in range(N_DP // 2):
                even = fresh[sweep, h, 2 * j].astype(F32)
                odd = fresh[sweep, h, 2 * j + 1].astype(F32)
                top = jnp.where(left, even, pltpu.roll(odd, 64, 1))
                bottom = jnp.where(left, pltpu.roll(even, 64, 1), odd)
                wide[:quarter, 128 * j : 128 * (j + 1)] = top
                wide[quarter:, 128 * j : 128 * (j + 1)] = bottom
                top_squares += top * top
                bottom_squares += bottom * bottom
            top_scale = lax.rsqrt(jnp.sum(top_squares, axis=1, keepdims=True) / D + EPSILON)
            bottom_scale = lax.rsqrt(jnp.sum(bottom_squares, axis=1, keepdims=True) / D + EPSILON)
            unit_cent[low_row:high_row] = (wide[:quarter] * top_scale).astype(BF16)
            unit_cent[high_row : half * (h + 1)] = (wide[quarter:] * bottom_scale).astype(BF16)

        def score(g, inner):
            distance = (g + 1) // 2
            origin = z + jnp.where(lax.rem(g, 2) == 1, -distance, distance)

            @pl.when(jnp.logical_and(origin >= 0, origin < N_Z))
            def _():
                @pl.when(sweep == 0)
                def _():
                    def arrive(i, deep):
                        sender = lax.rem(seat + i, LAYER)
                        slot = rows.at[origin * LAYER + sender]
                        pltpu.make_async_copy(
                            slot, slot, x_recv.at[origin * LAYER + sender]
                        ).wait()
                        return deep

                    lax.fori_loop(1, LAYER, arrive, 0)

                mine = rows[pl.ds(origin * LAYER, LAYER)].reshape(LAYER * CAP, D)
                scores = lax.dot_general(
                    unit_cent[...], mine, (((1,), (1,)), ((), ())), preferred_element_type=F32
                )
                weights = jnp.exp(scores * (SHARPNESS / D))
                raw[:, lanes(origin * LAYER * CAP, LAYER * CAP)] = weights
                added = jnp.sum(weights, axis=0, keepdims=True)
                for j in range(N_X):
                    part[sweep, j, pl.ds(origin, 1), :] = added[:, 128 * j : 128 * (j + 1)]

            return inner

        lax.fori_loop(0, 2 * N_Z - 1, score, 0)

        exchange_seats(part, part_in, sweep, part_send, part_recv)
        parts = split(take_halves(part_in, sweep))
        by_row = jnp.zeros((LAYER, ROWS), F32)
        for layer in range(N_Z):
            product = jnp.dot(parts, picks[layer], preferred_element_type=F32)
            by_row += own_row(product, layer)
        line_in[sweep, z] = by_row[:N_Z]

        def send_line(i, inner):
            line_copy(sweep, i).start()
            return inner

        lax.fori_loop(1, N_Z, send_line, 0)
        seen = line_in.at[sweep, pl.ds(0, N_Z - 1)]
        pltpu.make_async_copy(seen, seen, line_recv.at[sweep]).wait()
        row_totals = line_in[sweep, 0]
        for layer in range(1, N_Z):
            row_totals += line_in[sweep, layer]
        parts = split(row_totals)
        by_slot = jnp.zeros((LAYER, LAYER * CAP), F32)
        for layer in range(N_Z):
            product = lax.dot_general(
                parts, picks[layer], (((1,), (1,)), ((), ())), preferred_element_type=F32
            )
            by_slot += own_row(product, layer)
        for j in range(N_X):
            total[sweep, j] = by_slot[:N_Z, 128 * j : 128 * (j + 1)]
        exchange_seats(total, total_in, sweep, total_send, total_recv)
        totals = take_halves(total_in, sweep)
        live = totals > 0.0
        inverse = jnp.where(live, 1.0 / jnp.where(live, totals, 1.0), 0.0)

        mass_part = jnp.zeros((BLOCK, 128), F32)
        for layer in range(N_Z):
            for j in range(N_X):
                start = layer * LAYER * CAP + 128 * j
                piece = slice(start, start + 128)
                shares = raw[:, piece] * inverse[layer : layer + 1, 128 * j : 128 * (j + 1)]
                low[:, piece] = shares.astype(BF16)
                mass_part += shares
        mass_row = jnp.sum(jnp.transpose(mass_part), axis=0, keepdims=True)
        for h in range(2):
            edge_out[sweep, h, 1:2, :] = mass_row[:, half * h : half * (h + 1)]

        def sum_step(i, inner):
            j = lax.rem(dp // 4 + i, N_DP // 4)
            block_rows = rows[:, :, lanes(j * 256, 256)].reshape(SLOTS, 256)
            sums = jnp.dot(low[...], block_rows, preferred_element_type=F32)
            for h in range(2):
                for k in range(2):
                    top = sums[half * h : half * h + quarter, 128 * k : 128 * (k + 1)]
                    bottom = sums[half * h + quarter : half * (h + 1), 128 * k : 128 * (k + 1)]
                    even = jnp.where(left, top, pltpu.roll(bottom, 64, 1))
                    odd = jnp.where(left, pltpu.roll(top, 64, 1), bottom)
                    panel_out[sweep, h, 4 * j + 2 * k] = even.astype(BF16)
                    panel_out[sweep, h, 4 * j + 2 * k + 1] = odd.astype(BF16)
            for k in range(4):
                target = 4 * j + lax.rem(dp + k, 4)

                @pl.when(target != dp)
                def _():
                    panel_copy(sweep, 0, target).start()

            return inner

        lax.fori_loop(0, N_DP // 4, sum_step, 0)

        def send_second(i, inner):
            panel_copy(sweep, 1, dp_peer(i)).start()
            return inner

        lax.fori_loop(1, N_DP, send_second, 0)

        for h in range(2):
            panel_in[sweep, h, dp] = panel_out[sweep, h, dp]
            seen = panel_in.at[sweep, h, pl.ds(0, N_DP - 1)]
            pltpu.make_async_copy(seen, seen, panel_recv.at[sweep, h]).wait()
            sums_panel = panel_in[sweep, h, 0].astype(F32)
            for j in range(1, N_DP):
                sums_panel += panel_in[sweep, h, j].astype(F32)

            squares = sums_panel * sums_panel
            squares = jnp.transpose(jnp.concatenate([squares, squares], axis=0))
            edge_out[sweep, h, 0:1, :] = jnp.where(
                left_row,
                jnp.sum(squares[:PANEL], axis=0, keepdims=True),
                jnp.sum(squares[PANEL:], axis=0, keepdims=True),
            )

            def send_edge(i, inner):
                edge_copy(sweep, h, i).start()
                return inner

            lax.fori_loop(1, N_DP, send_edge, 0)
            edge_in[sweep, h, dp] = edge_out[sweep, h]
            seen = edge_in.at[sweep, h, pl.ds(0, N_DP - 1)]
            pltpu.make_async_copy(seen, seen, edge_recv.at[sweep, h]).wait()
            edges = edge_in[sweep, h, 0]
            for j in range(1, N_DP):
                edges += edge_in[sweep, h, j]
            scales = lax.rsqrt(edges[0:1] / D + EPSILON)
            turned = pltpu.roll(scales, 64, 1)
            scale_t = jnp.concatenate(
                [
                    jnp.broadcast_to(jnp.where(left_row, scales, turned), (PANEL, 128)),
                    jnp.broadcast_to(jnp.where(left_row, turned, scales), (PANEL, 128)),
                ],
                axis=0,
            )
            new_panel = sums_panel * jnp.transpose(scale_t)[:quarter]

            @pl.when(sweep < ITERS - 1)
            def _():
                fresh[sweep + 1, h, dp] = new_panel.astype(BF16)

                def send_fresh(i, inner):
                    fresh_copy(sweep + 1, h, i).start()
                    return inner

                lax.fori_loop(1, N_DP, send_fresh, 0)

            @pl.when(sweep == ITERS - 1)
            def _():
                out_ref[half * h : half * h + quarter] = new_panel[:, :PANEL]
                out_ref[half * h + quarter : half * (h + 1)] = new_panel[:, PANEL:]
                mass_ref[:, half * h : half * (h + 1)] = edges[1:2]

        return carry

    lax.fori_loop(0, ITERS, sweep_step, 0)

    def leave(sweep, carry):
        for ref, sem, count in (
            (part_in, part_send, LAYER - 1),
            (line_in, line_send, N_Z - 1),
            (total_in, total_send, LAYER - 1),
        ):
            sent = ref.at[sweep, pl.ds(0, count)]
            pltpu.make_async_copy(sent, sent, sem.at[sweep]).wait()
        for h in range(2):
            for ref, sem in ((panel_in, panel_send), (edge_in, edge_send)):
                sent = ref.at[sweep, h, pl.ds(0, N_DP - 1)]
                pltpu.make_async_copy(sent, sent, sem.at[sweep, h]).wait()
        return carry

    lax.fori_loop(0, ITERS, leave, 0)
    for h in range(2):
        sent = fresh.at[1, h, pl.ds(0, N_DP - 1)]
        pltpu.make_async_copy(sent, sent, fresh_send.at[h]).wait()
    pair_copy.wait_send()
    sent = fresh.at[0, :, pl.ds(0, 2 * (N_Y - 1))]
    pltpu.make_async_copy(sent, sent, first_sems.at[0]).wait()

    def leave_origin(origin, carry):
        def step(i, inner):
            row_copy(origin, i).wait_send()
            return inner

        lax.fori_loop(1, LAYER, step, 0)

        @pl.when(jnp.logical_and(origin <= z, z < N_Z - 1))
        def _():
            unit_copy(origin, 1).wait_send()

        @pl.when(jnp.logical_and(origin >= z, z > 0))
        def _():
            unit_copy(origin, 0).wait_send()

        @pl.when(origin != z)
        def _():
            rank_copy(origin).wait_send()

        return carry

    lax.fori_loop(0, N_Z, leave_origin, 0)


def body(vectors, candidates, centroids):
    vmem = pl.BlockSpec(memory_space=pltpu.VMEM)
    dma = pltpu.SemaphoreType.DMA
    panel, mass = pl.pallas_call(
        kernel,
        out_shape=(
            jax.ShapeDtypeStruct((BLOCK, PANEL), F32),
            jax.ShapeDtypeStruct((1, BLOCK), F32),
        ),
        in_specs=[vmem] * 3,
        out_specs=(vmem, vmem),
        scratch_shapes=[
            pltpu.VMEM((N_Z, ROWS, D), BF16),
            pltpu.VMEM((N_Z, 2, LAYER, ROWS), jnp.int32),
            pltpu.VMEM((N_Z, LAYER * CAP, ROWS), BF16),
            pltpu.VMEM((N_Z, LAYER, CAP, D), BF16),
            pltpu.VMEM((N_CENT, CAP, D), BF16),
            pltpu.VMEM((BLOCK, SLOTS), F32),
            pltpu.VMEM((BLOCK, SLOTS), BF16),
            pltpu.VMEM((ITERS, N_X, N_Z, 128), F32),
            pltpu.VMEM((ITERS, LAYER, N_Z, 128), F32),
            pltpu.VMEM((ITERS, N_Z, N_Z, ROWS), F32),
            pltpu.VMEM((ITERS, N_X, N_Z, 128), F32),
            pltpu.VMEM((ITERS, LAYER, N_Z, 128), F32),
            pltpu.VMEM((BLOCK // 2, D), F32),
            pltpu.VMEM((BLOCK, D), BF16),
            pltpu.VMEM((ITERS, 2, N_DP, BLOCK // 4, 128), BF16),
            pltpu.VMEM((ITERS, 2, N_DP, BLOCK // 4, 128), BF16),
            pltpu.VMEM((ITERS, 2, N_DP, BLOCK // 4, 128), BF16),
            pltpu.VMEM((ITERS, 2, 2, 128), F32),
            pltpu.VMEM((ITERS, 2, N_DP, 2, 128), F32),
            dma((N_Z, 2)),
            dma((N_Z,)),
            dma((N_Z,)),
            dma((N_Z,)),
            dma((N_Z, LAYER)),
            dma((N_CENT,)),
            dma((2,)),
            dma((2,)),
            dma((ITERS,)),
            dma((ITERS,)),
            dma((ITERS,)),
            dma((ITERS,)),
            dma((ITERS,)),
            dma((ITERS,)),
            dma((ITERS, 2)),
            dma((ITERS, 2)),
            dma((2,)),
            dma((2,)),
            dma((ITERS, 2)),
            dma((ITERS, 2)),
        ],
        compiler_params=pltpu.CompilerParams(
            collective_id=0, has_side_effects=True, vmem_limit_bytes=48 * 1024 * 1024
        ),
        cost_estimate=pl.CostEstimate(
            flops=9 * 2 * SLOTS * BLOCK * D // 2, bytes_accessed=4 << 20, transcendentals=SLOTS * BLOCK
        ),
        name="soft_kmeans",
    )(vectors, candidates.T, centroids)
    return panel, mass.reshape(BLOCK)


def solution(mesh):
    return jax.shard_map(
        body,
        mesh=mesh,
        in_specs=(P(("dp", "cent"), None), P(("dp", "cent"), None), P("cent", "dp")),
        out_specs=(P("cent", "dp"), P("cent")),
        check_vma=False,
    )
```

```python
import functools

import jax
import jax.numpy as jnp
from jax import lax
from jax.experimental import pallas as pl
from jax.experimental.pallas import tpu as pltpu
from jax.sharding import PartitionSpec as P

ITERS = 2
EPSILON = 1e-06
SHARPNESS = 20.0

D = 1024
ROWS = 256
BLOCK = 256
CAP = 64
N_DP = 16
N_CENT = 32
N_X = 4
N_Y = 8
N_Z = 4
LAYER = 8
SLOTS = N_CENT * CAP
PANEL = D // N_DP

F32 = jnp.float32
BF16 = jnp.bfloat16
MESH = pl.DeviceIdType.MESH


def lanes(start, size):
    return pl.ds(pl.multiple_of(start, 128), size)


def kernel(
    vec_ref,
    cand_ref,
    cent_ref,
    out_ref,
    mass_ref,
    units,
    ranks,
    picks,
    packed,
    rows,
    raw,
    low,
    part,
    part_in,
    line_in,
    total,
    total_in,
    wide,
    unit_cent,
    panel_out,
    panel_in,
    fresh,
    last_sums,
    edge_out,
    edge_in,
    vouched,
    z_send,
    z_recv,
    rank_send,
    rank_recv,
    x_send,
    x_recv,
    pair_sems,
    first_sems,
    part_send,
    part_recv,
    line_send,
    line_recv,
    total_send,
    total_recv,
    panel_send,
    panel_recv,
    fresh_send,
    fresh_recv,
    edge_send,
    edge_recv,
):
    dp = lax.axis_index("dp")
    cent = lax.axis_index("cent")
    x = cent // LAYER
    z = (cent // 2) % N_Z
    core = cent % 2
    seat = x * 2 + core

    def dp_peer(i):
        return lax.rem(dp + i, N_DP)

    def y_peer(i):
        return (dp // N_Y) * N_Y + lax.rem(dp + i, N_Y)

    other_dp = lax.rem(dp + N_Y, N_DP)

    def seat_peer(i):
        return lax.rem(seat + i, LAYER)

    def z_peer(i):
        return lax.rem(z + i, N_Z)

    def at_seat(other):
        return (dp, (other // 2) * LAYER + z * 2 + other % 2)

    def at_layer(other):
        return (dp, x * LAYER + other * 2 + core)

    barrier = pltpu.get_barrier_semaphore()

    def greet_seat(i, carry):
        pl.semaphore_signal(barrier, inc=1, device_id=at_seat(seat_peer(i)), device_id_type=MESH)
        return carry

    def greet_layer(i, carry):
        pl.semaphore_signal(barrier, inc=1, device_id=at_layer(z_peer(i)), device_id_type=MESH)
        return carry

    def greet_y(i, carry):
        pl.semaphore_signal(barrier, inc=1, device_id=(y_peer(i), cent), device_id_type=MESH)
        return carry

    lax.fori_loop(1, LAYER, greet_seat, 0)
    lax.fori_loop(1, N_Z, greet_layer, 0)
    lax.fori_loop(1, N_Y, greet_y, 0)
    pl.semaphore_signal(barrier, inc=1, device_id=(other_dp, cent), device_id_type=MESH)

    vec = vec_ref[...].astype(F32)
    vec_scale = lax.rsqrt(jnp.mean(vec * vec, axis=1, keepdims=True) + EPSILON)
    units[z] = (vec * vec_scale).astype(BF16)
    cand = cand_ref[...]
    place = lax.broadcasted_iota(jnp.int32, (N_CENT, ROWS), 0)
    block = ((place >> 1) & (N_X - 1)) * LAYER + (place >> 3) * 2 + (place & 1)
    named = cand[0:1, :] == block
    for j in range(1, cand.shape[0]):
        named = jnp.logical_or(named, cand[j : j + 1, :] == block)
    named_f = jnp.where(named, 1.0, 0.0)
    first = lax.broadcasted_iota(jnp.int32, (ROWS, ROWS), 0)
    second = lax.broadcasted_iota(jnp.int32, (ROWS, ROWS), 1)
    before = jnp.where(first < second, 1.0, 0.0).astype(BF16)
    rank = jnp.dot(named_f.astype(BF16), before, preferred_element_type=F32)
    slots = jnp.where(named, rank, -1.0).astype(jnp.int32)
    for layer in range(N_Z):
        ranks[layer, 0] = slots[layer * LAYER : (layer + 1) * LAYER]

    slot_iota = lax.broadcasted_iota(jnp.int32, (CAP, ROWS), 0)

    def pick_rows(rank_rows):
        picks = [
            jnp.where(rank_rows[j : j + 1, :] == slot_iota, 1.0, 0.0).astype(BF16)
            for j in range(LAYER)
        ]
        return jnp.concatenate(picks, axis=0)

    def pack(origin, rank_rows):
        picks[origin] = pick_rows(rank_rows)
        chosen = jnp.dot(picks[origin], units[origin], preferred_element_type=F32)
        packed[origin] = chosen.astype(BF16).reshape(LAYER, CAP, D)
        rows[origin * LAYER + seat] = packed[origin, seat]

    panel0 = cent_ref[...]
    half = BLOCK // 2
    quarter = half // 2
    for h in range(2):
        fresh[0, h, dp] = jnp.concatenate(
            [panel0[half * h : half * h + quarter], panel0[half * h + quarter : half * (h + 1)]],
            axis=1,
        )

    pack(z, ranks[z, 0])

    pl.semaphore_wait(barrier, LAYER - 1 + N_Z - 1 + N_Y)
    pl.semaphore_signal(vouched, inc=1, device_id=(other_dp, cent), device_id_type=MESH)

    def rank_copy(layer):
        return pltpu.make_async_remote_copy(
            src_ref=ranks.at[layer, 0],
            dst_ref=ranks.at[z, 1],
            send_sem=rank_send.at[layer],
            recv_sem=rank_recv.at[z],
            device_id=at_layer(layer),
            device_id_type=MESH,
        )

    def unit_copy(origin, side):
        return pltpu.make_async_remote_copy(
            src_ref=units.at[origin],
            dst_ref=units.at[origin],
            send_sem=z_send.at[origin, side],
            recv_sem=z_recv.at[origin],
            device_id=at_layer(z + 2 * side - 1),
            device_id_type=MESH,
        )

    def start_up(origin):
        @pl.when(z < N_Z - 1)
        def _():
            unit_copy(origin, 1).start()

    def start_down(origin):
        @pl.when(z > 0)
        def _():
            unit_copy(origin, 0).start()

    start_up(z)
    start_down(z)

    def send_rank(i, carry):
        rank_copy(z_peer(i)).start()
        return carry

    lax.fori_loop(1, N_Z, send_rank, 0)

    pair_copy = pltpu.make_async_remote_copy(
        src_ref=fresh.at[0, :, dp],
        dst_ref=fresh.at[0, :, dp],
        send_sem=pair_sems.at[0],
        recv_sem=pair_sems.at[1],
        device_id=(other_dp, cent),
        device_id_type=MESH,
    )
    pair_copy.start()

    def first_copy(which, i):
        return pltpu.make_async_remote_copy(
            src_ref=fresh.at[0, :, which],
            dst_ref=fresh.at[0, :, which],
            send_sem=first_sems.at[0],
            recv_sem=first_sems.at[1],
            device_id=(y_peer(i), cent),
            device_id_type=MESH,
        )

    def fresh_copy(sweep, h, i):
        return pltpu.make_async_remote_copy(
            src_ref=fresh.at[sweep, h, dp],
            dst_ref=fresh.at[sweep, h, dp],
            send_sem=fresh_send.at[h],
            recv_sem=fresh_recv.at[h],
            device_id=(dp_peer(i), cent),
            device_id_type=MESH,
        )

    def row_copy(origin, i):
        target = seat_peer(i)
        return pltpu.make_async_remote_copy(
            src_ref=packed.at[origin, target],
            dst_ref=rows.at[origin * LAYER + seat],
            send_sem=x_send.at[origin, target],
            recv_sem=x_recv.at[origin * LAYER + seat],
            device_id=at_seat(target),
            device_id_type=MESH,
        )

    def send_packed(origin):
        def step(i, carry):
            row_copy(origin, i).start()
            return carry

        lax.fori_loop(1, LAYER, step, 0)

    send_packed(z)

    pair_copy.wait_recv()

    def send_first(i, carry):
        first_copy(dp, i).start()
        first_copy(other_dp, i).start()
        return carry

    lax.fori_loop(1, N_Y, send_first, 0)

    def event(e, carry):
        distance = (e + 1) // 2
        up = lax.rem(e, 2)
        origin = z + jnp.where(up == 1, -distance, distance)

        @pl.when(jnp.logical_and(origin >= 0, origin < N_Z))
        def _():
            unit_copy(origin, 0).wait_recv()

            @pl.when(up == 1)
            def _():
                start_up(origin)

            @pl.when(up == 0)
            def _():
                start_down(origin)

            rank_copy_in(origin).wait_recv()
            pack(origin, ranks[origin, 1])
            send_packed(origin)

        return carry

    def rank_copy_in(origin):
        return pltpu.make_async_remote_copy(
            src_ref=ranks.at[origin, 0],
            dst_ref=ranks.at[origin, 1],
            send_sem=rank_send.at[origin],
            recv_sem=rank_recv.at[origin],
            device_id=at_layer(origin),
            device_id_type=MESH,
        )

    lax.fori_loop(1, 2 * N_Z - 1, event, 0)
    pl.semaphore_wait(vouched, 1)

    left = lax.broadcasted_iota(jnp.int32, (quarter, 128), 1) < PANEL
    left_four = lax.broadcasted_iota(jnp.int32, (N_Z, 128), 1) < CAP
    left_row = lax.broadcasted_iota(jnp.int32, (1, 128), 1) < PANEL
    layer_iota = lax.broadcasted_iota(jnp.int32, (LAYER, 1), 0)

    def take_halves(ref, sweep):
        pieces = []
        for j in range(LAYER // 2):
            even = ref[sweep, 2 * j]
            odd = ref[sweep, 2 * j + 1]
            first_core = jnp.where(left_four, even, pltpu.roll(odd, 64, 1))
            second_core = jnp.where(left_four, pltpu.roll(even, 64, 1), odd)
            pieces.append(jnp.where(core == 0, first_core, second_core))
        return jnp.concatenate(pieces, axis=1)

    def split(four):
        zeros = jnp.zeros((LAYER - N_Z, four.shape[1]), F32)
        value = jnp.concatenate([four, zeros], axis=0)
        high = value.astype(BF16).astype(F32)
        rest = value - high
        middle = rest.astype(BF16).astype(F32)
        return jnp.concatenate([high, middle, rest - middle], axis=0).astype(BF16)

    def own_row(product, layer):
        added = product[:LAYER] + product[LAYER : 2 * LAYER] + product[2 * LAYER :]
        return jnp.where(layer_iota == layer, added, 0.0)

    def seat_copy(source, target, sweep, i, send_sem, recv_sem):
        other = seat_peer(i)
        return pltpu.make_async_remote_copy(
            src_ref=source.at[sweep, other // 2],
            dst_ref=target.at[sweep, seat],
            send_sem=send_sem.at[sweep],
            recv_sem=recv_sem.at[sweep],
            device_id=at_seat(other),
            device_id_type=MESH,
        )

    def exchange_seats(source, target, sweep, send_sem, recv_sem):
        def step(i, carry):
            seat_copy(source, target, sweep, i, send_sem, recv_sem).start()
            return carry

        lax.fori_loop(1, LAYER, step, 0)
        target[sweep, seat] = source[sweep, x]
        seen = target.at[sweep, pl.ds(0, LAYER - 1)]
        pltpu.make_async_copy(seen, seen, recv_sem.at[sweep]).wait()

    def line_copy(sweep, i):
        return pltpu.make_async_remote_copy(
            src_ref=line_in.at[sweep, z],
            dst_ref=line_in.at[sweep, z],
            send_sem=line_send.at[sweep],
            recv_sem=line_recv.at[sweep],
            device_id=at_layer(z_peer(i)),
            device_id_type=MESH,
        )

    def edge_copy(h, i):
        return pltpu.make_async_remote_copy(
            src_ref=edge_out.at[h],
            dst_ref=edge_in.at[h, dp],
            send_sem=edge_send.at[h],
            recv_sem=edge_recv.at[h],
            device_id=(dp_peer(i), cent),
            device_id_type=MESH,
        )

    def panel_copy(sweep, h, target):
        return pltpu.make_async_remote_copy(
            src_ref=panel_out.at[sweep, h, target],
            dst_ref=panel_in.at[sweep, h, dp],
            send_sem=panel_send.at[sweep, h],
            recv_sem=panel_recv.at[sweep, h],
            device_id=(target, cent),
            device_id_type=MESH,
        )

    def unit_scale(squares, sweep):
        mean = jnp.sum(squares, axis=1, keepdims=True) / D
        scale = jnp.where(sweep == 0, 1.0, lax.rsqrt(mean + EPSILON))
        return scale * lax.rsqrt(mean * scale * scale + EPSILON)

    def sweep_step(sweep, carry):
        @pl.when(sweep == 0)
        def _():
            seen = fresh.at[0, :, pl.ds(0, 2 * (N_Y - 1))]
            pltpu.make_async_copy(seen, seen, first_sems.at[1]).wait()

        for h in range(2):
            @pl.when(sweep > 0)
            def _():
                seen = fresh.at[sweep, h, pl.ds(0, N_DP - 1)]
                pltpu.make_async_copy(seen, seen, fresh_recv.at[h]).wait()

            low_row, high_row = half * h, half * h + quarter
            top_squares = jnp.zeros((quarter, 128), F32)
            bottom_squares = jnp.zeros((quarter, 128), F32)
            for j in range(N_DP // 2):
                even = fresh[sweep, h, 2 * j].astype(F32)
                odd = fresh[sweep, h, 2 * j + 1].astype(F32)
                top = jnp.where(left, even, pltpu.roll(odd, 64, 1))
                bottom = jnp.where(left, pltpu.roll(even, 64, 1), odd)
                wide[:quarter, 128 * j : 128 * (j + 1)] = top
                wide[quarter:, 128 * j : 128 * (j + 1)] = bottom
                top_squares += top * top
                bottom_squares += bottom * bottom
            top_scale = unit_scale(top_squares, sweep)
            bottom_scale = unit_scale(bottom_squares, sweep)
            unit_cent[low_row:high_row] = (wide[:quarter] * top_scale).astype(BF16)
            unit_cent[high_row : half * (h + 1)] = (wide[quarter:] * bottom_scale).astype(BF16)

        def score(g, inner):
            distance = (g + 1) // 2
            origin = z + jnp.where(lax.rem(g, 2) == 1, -distance, distance)

            @pl.when(jnp.logical_and(origin >= 0, origin < N_Z))
            def _():
                @pl.when(sweep == 0)
                def _():
                    def arrive(i, deep):
                        sender = lax.rem(seat + i, LAYER)
                        slot = rows.at[origin * LAYER + sender]
                        pltpu.make_async_copy(
                            slot, slot, x_recv.at[origin * LAYER + sender]
                        ).wait()
                        return deep

                    lax.fori_loop(1, LAYER, arrive, 0)

                mine = rows[pl.ds(origin * LAYER, LAYER)].reshape(LAYER * CAP, D)
                scores = lax.dot_general(
                    unit_cent[...], mine, (((1,), (1,)), ((), ())), preferred_element_type=F32
                )
                weights = jnp.exp(scores * (SHARPNESS / D))
                raw[:, lanes(origin * LAYER * CAP, LAYER * CAP)] = weights
                added = jnp.sum(weights, axis=0, keepdims=True)
                for j in range(N_X):
                    part[sweep, j, pl.ds(origin, 1), :] = added[:, 128 * j : 128 * (j + 1)]

            return inner

        lax.fori_loop(0, 2 * N_Z - 1, score, 0)

        exchange_seats(part, part_in, sweep, part_send, part_recv)
        parts = split(take_halves(part_in, sweep))
        by_row = jnp.zeros((LAYER, ROWS), F32)
        for layer in range(N_Z):
            product = jnp.dot(parts, picks[layer], preferred_element_type=F32)
            by_row += own_row(product, layer)
        line_in[sweep, z] = by_row[:N_Z]

        def send_line(i, inner):
            line_copy(sweep, i).start()
            return inner

        lax.fori_loop(1, N_Z, send_line, 0)
        seen = line_in.at[sweep, pl.ds(0, N_Z - 1)]
        pltpu.make_async_copy(seen, seen, line_recv.at[sweep]).wait()
        row_totals = line_in[sweep, 0]
        for layer in range(1, N_Z):
            row_totals += line_in[sweep, layer]
        parts = split(row_totals)
        by_slot = jnp.zeros((LAYER, LAYER * CAP), F32)
        for layer in range(N_Z):
            product = lax.dot_general(
                parts, picks[layer], (((1,), (1,)), ((), ())), preferred_element_type=F32
            )
            by_slot += own_row(product, layer)
        for j in range(N_X):
            total[sweep, j] = by_slot[:N_Z, 128 * j : 128 * (j + 1)]
        exchange_seats(total, total_in, sweep, total_send, total_recv)
        totals = take_halves(total_in, sweep)
        live = totals > 0.0
        inverse = jnp.where(live, 1.0 / jnp.where(live, totals, 1.0), 0.0)

        mass_part = jnp.zeros((BLOCK, 128), F32)
        for layer in range(N_Z):
            for j in range(N_X):
                start = layer * LAYER * CAP + 128 * j
                piece = slice(start, start + 128)
                shares = raw[:, piece] * inverse[layer : layer + 1, 128 * j : 128 * (j + 1)]
                low[:, piece] = shares.astype(BF16)
                mass_part += shares
        mass_row = jnp.sum(jnp.transpose(mass_part), axis=0, keepdims=True)
        for h in range(2):
            edge_out[h, 1:2, :] = mass_row[:, half * h : half * (h + 1)]

        def sum_step(i, inner):
            j = lax.rem(dp // 4 + i, N_DP // 4)
            block_rows = rows[:, :, lanes(j * 256, 256)].reshape(SLOTS, 256)
            sums = jnp.dot(low[...], block_rows, preferred_element_type=F32)
            for h in range(2):
                for k in range(2):
                    top = sums[half * h : half * h + quarter, 128 * k : 128 * (k + 1)]
                    bottom = sums[half * h + quarter : half * (h + 1), 128 * k : 128 * (k + 1)]
                    even = jnp.where(left, top, pltpu.roll(bottom, 64, 1))
                    odd = jnp.where(left, pltpu.roll(top, 64, 1), bottom)
                    panel_out[sweep, h, 4 * j + 2 * k] = even.astype(BF16)
                    panel_out[sweep, h, 4 * j + 2 * k + 1] = odd.astype(BF16)
            for k in range(4):
                target = 4 * j + lax.rem(dp + k, 4)

                @pl.when(target != dp)
                def _():
                    panel_copy(sweep, 0, target).start()

            return inner

        lax.fori_loop(0, N_DP // 4, sum_step, 0)

        def send_second(i, inner):
            panel_copy(sweep, 1, dp_peer(i)).start()
            return inner

        lax.fori_loop(1, N_DP, send_second, 0)

        for h in range(2):
            panel_in[sweep, h, dp] = panel_out[sweep, h, dp]
            seen = panel_in.at[sweep, h, pl.ds(0, N_DP - 1)]
            pltpu.make_async_copy(seen, seen, panel_recv.at[sweep, h]).wait()
            sums_panel = panel_in[sweep, h, 0].astype(F32)
            for j in range(1, N_DP):
                sums_panel += panel_in[sweep, h, j].astype(F32)

            @pl.when(sweep < ITERS - 1)
            def _():
                fresh[sweep + 1, h, dp] = sums_panel.astype(BF16)

                def send_fresh(i, inner):
                    fresh_copy(sweep + 1, h, i).start()
                    return inner

                lax.fori_loop(1, N_DP, send_fresh, 0)

            @pl.when(sweep == ITERS - 1)
            def _():
                last_sums[h] = sums_panel
                squares = sums_panel * sums_panel
                squares = jnp.transpose(jnp.concatenate([squares, squares], axis=0))
                edge_out[h, 0:1, :] = jnp.where(
                    left_row,
                    jnp.sum(squares[:PANEL], axis=0, keepdims=True),
                    jnp.sum(squares[PANEL:], axis=0, keepdims=True),
                )

                def send_edge(i, inner):
                    edge_copy(h, i).start()
                    return inner

                lax.fori_loop(1, N_DP, send_edge, 0)
                edge_in[h, dp] = edge_out[h]

        return carry

    lax.fori_loop(0, ITERS, sweep_step, 0)

    for h in range(2):
        seen = edge_in.at[h, pl.ds(0, N_DP - 1)]
        pltpu.make_async_copy(seen, seen, edge_recv.at[h]).wait()
        edges = edge_in[h, 0]
        for j in range(1, N_DP):
            edges += edge_in[h, j]
        scales = lax.rsqrt(edges[0:1] / D + EPSILON)
        turned = pltpu.roll(scales, 64, 1)
        scale_t = jnp.concatenate(
            [
                jnp.broadcast_to(jnp.where(left_row, scales, turned), (PANEL, 128)),
                jnp.broadcast_to(jnp.where(left_row, turned, scales), (PANEL, 128)),
            ],
            axis=0,
        )
        new_panel = last_sums[h] * jnp.transpose(scale_t)[:quarter]
        out_ref[half * h : half * h + quarter] = new_panel[:, :PANEL]
        out_ref[half * h + quarter : half * (h + 1)] = new_panel[:, PANEL:]
        mass_ref[:, half * h : half * (h + 1)] = edges[1:2]

    def leave(sweep, carry):
        for ref, sem, count in (
            (part_in, part_send, LAYER - 1),
            (line_in, line_send, N_Z - 1),
            (total_in, total_send, LAYER - 1),
        ):
            sent = ref.at[sweep, pl.ds(0, count)]
            pltpu.make_async_copy(sent, sent, sem.at[sweep]).wait()
        for h in range(2):
            sent = panel_in.at[sweep, h, pl.ds(0, N_DP - 1)]
            pltpu.make_async_copy(sent, sent, panel_send.at[sweep, h]).wait()
        return carry

    lax.fori_loop(0, ITERS, leave, 0)
    for h in range(2):
        sent = fresh.at[1, h, pl.ds(0, N_DP - 1)]
        pltpu.make_async_copy(sent, sent, fresh_send.at[h]).wait()
        sent = edge_in.at[h, pl.ds(0, N_DP - 1)]
        pltpu.make_async_copy(sent, sent, edge_send.at[h]).wait()
    pair_copy.wait_send()
    sent = fresh.at[0, :, pl.ds(0, 2 * (N_Y - 1))]
    pltpu.make_async_copy(sent, sent, first_sems.at[0]).wait()

    def leave_origin(origin, carry):
        def step(i, inner):
            row_copy(origin, i).wait_send()
            return inner

        lax.fori_loop(1, LAYER, step, 0)

        @pl.when(jnp.logical_and(origin <= z, z < N_Z - 1))
        def _():
            unit_copy(origin, 1).wait_send()

        @pl.when(jnp.logical_and(origin >= z, z > 0))
        def _():
            unit_copy(origin, 0).wait_send()

        @pl.when(origin != z)
        def _():
            rank_copy(origin).wait_send()

        return carry

    lax.fori_loop(0, N_Z, leave_origin, 0)


def body(vectors, candidates, centroids):
    vmem = pl.BlockSpec(memory_space=pltpu.VMEM)
    dma = pltpu.SemaphoreType.DMA
    panel, mass = pl.pallas_call(
        kernel,
        out_shape=(
            jax.ShapeDtypeStruct((BLOCK, PANEL), F32),
            jax.ShapeDtypeStruct((1, BLOCK), F32),
        ),
        in_specs=[vmem] * 3,
        out_specs=(vmem, vmem),
        scratch_shapes=[
            pltpu.VMEM((N_Z, ROWS, D), BF16),
            pltpu.VMEM((N_Z, 2, LAYER, ROWS), jnp.int32),
            pltpu.VMEM((N_Z, LAYER * CAP, ROWS), BF16),
            pltpu.VMEM((N_Z, LAYER, CAP, D), BF16),
            pltpu.VMEM((N_CENT, CAP, D), BF16),
            pltpu.VMEM((BLOCK, SLOTS), F32),
            pltpu.VMEM((BLOCK, SLOTS), BF16),
            pltpu.VMEM((ITERS, N_X, N_Z, 128), F32),
            pltpu.VMEM((ITERS, LAYER, N_Z, 128), F32),
            pltpu.VMEM((ITERS, N_Z, N_Z, ROWS), F32),
            pltpu.VMEM((ITERS, N_X, N_Z, 128), F32),
            pltpu.VMEM((ITERS, LAYER, N_Z, 128), F32),
            pltpu.VMEM((BLOCK // 2, D), F32),
            pltpu.VMEM((BLOCK, D), BF16),
            pltpu.VMEM((ITERS, 2, N_DP, BLOCK // 4, 128), BF16),
            pltpu.VMEM((ITERS, 2, N_DP, BLOCK // 4, 128), BF16),
            pltpu.VMEM((ITERS, 2, N_DP, BLOCK // 4, 128), BF16),
            pltpu.VMEM((2, BLOCK // 4, 128), F32),
            pltpu.VMEM((2, 2, 128), F32),
            pltpu.VMEM((2, N_DP, 2, 128), F32),
            pltpu.SemaphoreType.REGULAR,
            dma((N_Z, 2)),
            dma((N_Z,)),
            dma((N_Z,)),
            dma((N_Z,)),
            dma((N_Z, LAYER)),
            dma((N_CENT,)),
            dma((2,)),
            dma((2,)),
            dma((ITERS,)),
            dma((ITERS,)),
            dma((ITERS,)),
            dma((ITERS,)),
            dma((ITERS,)),
            dma((ITERS,)),
            dma((ITERS, 2)),
            dma((ITERS, 2)),
            dma((2,)),
            dma((2,)),
            dma((2,)),
            dma((2,)),
        ],
        compiler_params=pltpu.CompilerParams(
            collective_id=0, has_side_effects=True, vmem_limit_bytes=48 * 1024 * 1024
        ),
        cost_estimate=pl.CostEstimate(
            flops=9 * 2 * SLOTS * BLOCK * D // 2, bytes_accessed=4 << 20, transcendentals=SLOTS * BLOCK
        ),
        name="soft_kmeans",
    )(vectors, candidates.T, centroids)
    return panel, mass.reshape(BLOCK)


def solution(mesh):
    return jax.shard_map(
        body,
        mesh=mesh,
        in_specs=(P(("dp", "cent"), None), P(("dp", "cent"), None), P("cent", "dp")),
        out_specs=(P("cent", "dp"), P("cent")),
        check_vma=False,
    )
```

```python
import functools

import jax
import jax.numpy as jnp
from jax import lax
from jax.experimental import pallas as pl
from jax.experimental.pallas import tpu as pltpu
from jax.sharding import PartitionSpec as P

ITERS = 2
EPSILON = 1e-06
SHARPNESS = 20.0

D = 1024
ROWS = 256
BLOCK = 256
CAP = 64
N_DP = 16
N_CENT = 32
N_X = 4
N_Y = 8
N_Z = 4
LAYER = 8
SLOTS = N_CENT * CAP
PANEL = D // N_DP

F32 = jnp.float32
BF16 = jnp.bfloat16
MESH = pl.DeviceIdType.MESH


def lanes(start, size):
    return pl.ds(pl.multiple_of(start, 128), size)


def kernel(
    vec_hbm,
    cand_hbm,
    cent_hbm,
    out_ref,
    mass_ref,
    vec_ref,
    cand_ref,
    cent_ref,
    fetch_sems,
    units,
    ranks,
    picks,
    packed,
    rows,
    raw,
    low,
    part,
    part_in,
    line_in,
    total,
    total_in,
    wide,
    unit_cent,
    panel_out,
    panel_in,
    fresh,
    last_sums,
    edge_out,
    edge_in,
    vouched,
    z_send,
    z_recv,
    rank_send,
    rank_recv,
    x_send,
    x_recv,
    pair_sems,
    first_sems,
    part_send,
    part_recv,
    line_send,
    line_recv,
    total_send,
    total_recv,
    panel_send,
    panel_recv,
    fresh_send,
    fresh_recv,
    edge_send,
    edge_recv,
):
    dp = lax.axis_index("dp")
    cent = lax.axis_index("cent")
    x = cent // LAYER
    z = (cent // 2) % N_Z
    core = cent % 2
    seat = x * 2 + core

    def offset(i):
        return 4 + i // 2 - lax.rem(i, 2) * (2 * (i // 2) + 1)

    def dp_peer(i):
        z_of = lax.rem(dp // N_Y + 1 - lax.rem(i, 2), 2)
        return z_of * N_Y + lax.rem(dp + offset(i // 2), N_Y)

    def y_peer(i):
        return (dp // N_Y) * N_Y + lax.rem(dp + offset(i), N_Y)

    other_dp = lax.rem(dp + N_Y, N_DP)

    def seat_peer(i):
        return lax.rem(seat + offset(i), LAYER)

    def z_peer(i):
        return lax.rem(z + i, N_Z)

    def at_seat(other):
        return (dp, (other // 2) * LAYER + z * 2 + other % 2)

    def at_layer(other):
        return (dp, x * LAYER + other * 2 + core)

    barrier = pltpu.get_barrier_semaphore()

    def greet_seat(i, carry):
        pl.semaphore_signal(barrier, inc=1, device_id=at_seat(seat_peer(i)), device_id_type=MESH)
        return carry

    def greet_layer(i, carry):
        pl.semaphore_signal(barrier, inc=1, device_id=at_layer(z_peer(i)), device_id_type=MESH)
        return carry

    def greet_y(i, carry):
        pl.semaphore_signal(barrier, inc=1, device_id=(y_peer(i), cent), device_id_type=MESH)
        return carry

    lax.fori_loop(0, LAYER - 1, greet_seat, 0)
    lax.fori_loop(1, N_Z, greet_layer, 0)
    lax.fori_loop(0, N_Y - 1, greet_y, 0)
    pl.semaphore_signal(barrier, inc=1, device_id=(other_dp, cent), device_id_type=MESH)

    fetches = [
        pltpu.make_async_copy(source, place, sem)
        for source, place, sem in (
            (vec_hbm, vec_ref, fetch_sems.at[0]),
            (cand_hbm, cand_ref, fetch_sems.at[1]),
            (cent_hbm, cent_ref, fetch_sems.at[2]),
        )
    ]
    for fetch in fetches:
        fetch.start()
    for fetch in fetches:
        fetch.wait()

    vec = vec_ref[...].astype(F32)
    vec_scale = lax.rsqrt(jnp.mean(vec * vec, axis=1, keepdims=True) + EPSILON)
    units[z] = (vec * vec_scale).astype(BF16)
    cand = cand_ref[...]
    place = lax.broadcasted_iota(jnp.int32, (N_CENT, ROWS), 0)
    block = ((place >> 1) & (N_X - 1)) * LAYER + (place >> 3) * 2 + (place & 1)
    named = cand[0:1, :] == block
    for j in range(1, cand.shape[0]):
        named = jnp.logical_or(named, cand[j : j + 1, :] == block)
    named_f = jnp.where(named, 1.0, 0.0)
    first = lax.broadcasted_iota(jnp.int32, (ROWS, ROWS), 0)
    second = lax.broadcasted_iota(jnp.int32, (ROWS, ROWS), 1)
    before = jnp.where(first < second, 1.0, 0.0).astype(BF16)
    rank = jnp.dot(named_f.astype(BF16), before, preferred_element_type=F32)
    slots = jnp.where(named, rank, -1.0).astype(jnp.int32)
    for layer in range(N_Z):
        ranks[layer, 0] = slots[layer * LAYER : (layer + 1) * LAYER]

    slot_iota = lax.broadcasted_iota(jnp.int32, (CAP, ROWS), 0)

    def pick_rows(rank_rows):
        picks = [
            jnp.where(rank_rows[j : j + 1, :] == slot_iota, 1.0, 0.0).astype(BF16)
            for j in range(LAYER)
        ]
        return jnp.concatenate(picks, axis=0)

    def pack(origin, rank_rows):
        picks[origin] = pick_rows(rank_rows)
        chosen = jnp.dot(picks[origin], units[origin], preferred_element_type=F32)
        packed[origin] = chosen.astype(BF16).reshape(LAYER, CAP, D)
        rows[origin * LAYER + seat] = packed[origin, seat]

    half = BLOCK // 2
    quarter = half // 2
    left = lax.broadcasted_iota(jnp.int32, (quarter, 128), 1) < PANEL
    for h in range(2):
        across = cent_ref[:, half * h : half * (h + 1)].astype(F32)
        along = jnp.transpose(jnp.concatenate([across, across], axis=0))
        fresh[0, h, dp] = jnp.where(left, along[:quarter], along[quarter:]).astype(BF16)

    pack(z, ranks[z, 0])

    pl.semaphore_wait(barrier, LAYER - 1 + N_Z - 1 + N_Y)
    pl.semaphore_signal(vouched, inc=1, device_id=(other_dp, cent), device_id_type=MESH)

    pair_copy = pltpu.make_async_remote_copy(
        src_ref=fresh.at[0, :, dp],
        dst_ref=fresh.at[0, :, dp],
        send_sem=pair_sems.at[0],
        recv_sem=pair_sems.at[1],
        device_id=(other_dp, cent),
        device_id_type=MESH,
    )
    pair_copy.start()

    def rank_copy(layer):
        return pltpu.make_async_remote_copy(
            src_ref=ranks.at[layer, 0],
            dst_ref=ranks.at[z, 1],
            send_sem=rank_send.at[layer],
            recv_sem=rank_recv.at[z],
            device_id=at_layer(layer),
            device_id_type=MESH,
        )

    def unit_copy(origin, side):
        return pltpu.make_async_remote_copy(
            src_ref=units.at[origin],
            dst_ref=units.at[origin],
            send_sem=z_send.at[origin, side],
            recv_sem=z_recv.at[origin],
            device_id=at_layer(z + 2 * side - 1),
            device_id_type=MESH,
        )

    def start_up(origin):
        @pl.when(z < N_Z - 1)
        def _():
            unit_copy(origin, 1).start()

    def start_down(origin):
        @pl.when(z > 0)
        def _():
            unit_copy(origin, 0).start()

    start_up(z)
    start_down(z)

    def send_rank(i, carry):
        rank_copy(z_peer(i)).start()
        return carry

    lax.fori_loop(1, N_Z, send_rank, 0)


    def first_copy(which, i):
        return pltpu.make_async_remote_copy(
            src_ref=fresh.at[0, :, which],
            dst_ref=fresh.at[0, :, which],
            send_sem=first_sems.at[0],
            recv_sem=first_sems.at[1],
            device_id=(y_peer(i), cent),
            device_id_type=MESH,
        )

    def fresh_copy(sweep, h, i):
        return pltpu.make_async_remote_copy(
            src_ref=fresh.at[sweep, h, dp],
            dst_ref=fresh.at[sweep, h, dp],
            send_sem=fresh_send.at[h],
            recv_sem=fresh_recv.at[h],
            device_id=(dp_peer(i), cent),
            device_id_type=MESH,
        )

    def row_copy(origin, i):
        target = seat_peer(i)
        return pltpu.make_async_remote_copy(
            src_ref=packed.at[origin, target],
            dst_ref=rows.at[origin * LAYER + seat],
            send_sem=x_send.at[origin, target],
            recv_sem=x_recv.at[origin * LAYER + seat],
            device_id=at_seat(target),
            device_id_type=MESH,
        )

    def send_packed(origin):
        def step(i, carry):
            row_copy(origin, i).start()
            return carry

        lax.fori_loop(0, LAYER - 1, step, 0)

    send_packed(z)

    def event(e, carry):
        distance = (e + 1) // 2
        up = lax.rem(e, 2)
        origin = z + jnp.where(up == 1, -distance, distance)

        @pl.when(jnp.logical_and(origin >= 0, origin < N_Z))
        def _():
            unit_copy(origin, 0).wait_recv()

            @pl.when(up == 1)
            def _():
                start_up(origin)

            @pl.when(up == 0)
            def _():
                start_down(origin)

            rank_copy_in(origin).wait_recv()
            pack(origin, ranks[origin, 1])
            send_packed(origin)

        return carry

    def rank_copy_in(origin):
        return pltpu.make_async_remote_copy(
            src_ref=ranks.at[origin, 0],
            dst_ref=ranks.at[origin, 1],
            send_sem=rank_send.at[origin],
            recv_sem=rank_recv.at[origin],
            device_id=at_layer(origin),
            device_id_type=MESH,
        )

    lax.fori_loop(1, 3, event, 0)
    pair_copy.wait_recv()

    def send_first(i, carry):
        first_copy(dp, i).start()
        first_copy(other_dp, i).start()
        return carry

    lax.fori_loop(0, N_Y - 1, send_first, 0)
    lax.fori_loop(3, 2 * N_Z - 1, event, 0)
    pl.semaphore_wait(vouched, 1)

    left_four = lax.broadcasted_iota(jnp.int32, (N_Z, 128), 1) < CAP
    layer_iota = lax.broadcasted_iota(jnp.int32, (LAYER, 1), 0)

    def take_halves(ref, sweep):
        pieces = []
        for j in range(LAYER // 2):
            even = ref[sweep, 2 * j]
            odd = ref[sweep, 2 * j + 1]
            first_core = jnp.where(left_four, even, pltpu.roll(odd, 64, 1))
            second_core = jnp.where(left_four, pltpu.roll(even, 64, 1), odd)
            pieces.append(jnp.where(core == 0, first_core, second_core))
        return jnp.concatenate(pieces, axis=1)

    def split(four):
        zeros = jnp.zeros((LAYER - N_Z, four.shape[1]), F32)
        value = jnp.concatenate([four, zeros], axis=0)
        high = value.astype(BF16).astype(F32)
        rest = value - high
        middle = rest.astype(BF16).astype(F32)
        return jnp.concatenate([high, middle, rest - middle], axis=0).astype(BF16)

    def own_row(product, layer):
        added = product[:LAYER] + product[LAYER : 2 * LAYER] + product[2 * LAYER :]
        return jnp.where(layer_iota == layer, added, 0.0)

    def seat_copy(source, target, sweep, i, send_sem, recv_sem):
        other = seat_peer(i)
        return pltpu.make_async_remote_copy(
            src_ref=source.at[sweep, other // 2],
            dst_ref=target.at[sweep, seat],
            send_sem=send_sem.at[sweep],
            recv_sem=recv_sem.at[sweep],
            device_id=at_seat(other),
            device_id_type=MESH,
        )

    def exchange_seats(source, target, sweep, send_sem, recv_sem):
        def step(i, carry):
            seat_copy(source, target, sweep, i, send_sem, recv_sem).start()
            return carry

        lax.fori_loop(0, LAYER - 1, step, 0)
        target[sweep, seat] = source[sweep, x]
        seen = target.at[sweep, pl.ds(0, LAYER - 1)]
        pltpu.make_async_copy(seen, seen, recv_sem.at[sweep]).wait()

    def line_copy(sweep, i):
        return pltpu.make_async_remote_copy(
            src_ref=line_in.at[sweep, z],
            dst_ref=line_in.at[sweep, z],
            send_sem=line_send.at[sweep],
            recv_sem=line_recv.at[sweep],
            device_id=at_layer(z_peer(i)),
            device_id_type=MESH,
        )

    def edge_copy(h, i):
        return pltpu.make_async_remote_copy(
            src_ref=edge_out.at[h],
            dst_ref=edge_in.at[h, dp],
            send_sem=edge_send.at[h],
            recv_sem=edge_recv.at[h],
            device_id=(dp_peer(i), cent),
            device_id_type=MESH,
        )

    def panel_copy(sweep, h, target):
        return pltpu.make_async_remote_copy(
            src_ref=panel_out.at[sweep, h, target],
            dst_ref=panel_in.at[sweep, h, dp],
            send_sem=panel_send.at[sweep, h],
            recv_sem=panel_recv.at[sweep, h],
            device_id=(target, cent),
            device_id_type=MESH,
        )

    def unit_scale(squares, sweep):
        mean = jnp.sum(squares, axis=1, keepdims=True) / D
        scale = jnp.where(sweep == 0, 1.0, lax.rsqrt(mean + EPSILON))
        return scale * lax.rsqrt(mean * scale * scale + EPSILON)

    def sweep_step(sweep, carry):
        def unit_half(h):
            low_row, high_row = half * h, half * h + quarter
            top_squares = jnp.zeros((quarter, 128), F32)
            bottom_squares = jnp.zeros((quarter, 128), F32)
            for j in range(N_DP // 2):
                even = fresh[sweep, h, 2 * j].astype(F32)
                odd = fresh[sweep, h, 2 * j + 1].astype(F32)
                top = jnp.where(left, even, pltpu.roll(odd, 64, 1))
                bottom = jnp.where(left, pltpu.roll(even, 64, 1), odd)
                wide[:quarter, 128 * j : 128 * (j + 1)] = top
                wide[quarter:, 128 * j : 128 * (j + 1)] = bottom
                top_squares += top * top
                bottom_squares += bottom * bottom
            top_scale = unit_scale(top_squares, sweep)
            bottom_scale = unit_scale(bottom_squares, sweep)
            unit_cent[low_row:high_row] = (wide[:quarter] * top_scale).astype(BF16)
            unit_cent[high_row : half * (h + 1)] = (wide[quarter:] * bottom_scale).astype(BF16)

        def score(origin, start, size):
            mine = rows[pl.ds(origin * LAYER, LAYER)].reshape(LAYER * CAP, D)
            scores = lax.dot_general(
                unit_cent[start : start + size],
                mine,
                (((1,), (1,)), ((), ())),
                preferred_element_type=F32,
            )
            weights = jnp.exp(scores * (SHARPNESS / D))
            raw[start : start + size, lanes(origin * LAYER * CAP, LAYER * CAP)] = weights
            added = jnp.sum(weights, axis=0, keepdims=True)
            for j in range(N_X):
                piece = added[:, 128 * j : 128 * (j + 1)]
                if start > 0:
                    piece += part[sweep, j, pl.ds(origin, 1), :]
                part[sweep, j, pl.ds(origin, 1), :] = piece

        @pl.when(sweep == 0)
        def _():
            seen = fresh.at[0, :, pl.ds(0, 2 * (N_Y - 1))]
            pltpu.make_async_copy(seen, seen, first_sems.at[1]).wait()
            for h in range(2):
                unit_half(h)

            def score_arrived(g, inner):
                distance = (g + 1) // 2
                origin = z + jnp.where(lax.rem(g, 2) == 1, -distance, distance)

                @pl.when(jnp.logical_and(origin >= 0, origin < N_Z))
                def _():
                    def arrive(i, deep):
                        sender = seat_peer(i)
                        slot = rows.at[origin * LAYER + sender]
                        pltpu.make_async_copy(
                            slot, slot, x_recv.at[origin * LAYER + sender]
                        ).wait()
                        return deep

                    lax.fori_loop(0, LAYER - 1, arrive, 0)
                    score(origin, 0, BLOCK)

                return inner

            lax.fori_loop(0, 2 * N_Z - 1, score_arrived, 0)

        @pl.when(sweep > 0)
        def _():
            for h in range(2):
                seen = fresh.at[sweep, h, pl.ds(0, N_DP - 1)]
                pltpu.make_async_copy(seen, seen, fresh_recv.at[h]).wait()
                unit_half(h)

                def score_half(origin, inner):
                    score(origin, half * h, half)
                    return inner

                lax.fori_loop(0, N_Z, score_half, 0)

        exchange_seats(part, part_in, sweep, part_send, part_recv)
        parts = split(take_halves(part_in, sweep))
        by_row = jnp.zeros((LAYER, ROWS), F32)
        for layer in range(N_Z):
            product = jnp.dot(parts, picks[layer], preferred_element_type=F32)
            by_row += own_row(product, layer)
        line_in[sweep, z] = by_row[:N_Z]

        def send_line(i, inner):
            line_copy(sweep, i).start()
            return inner

        lax.fori_loop(1, N_Z, send_line, 0)
        seen = line_in.at[sweep, pl.ds(0, N_Z - 1)]
        pltpu.make_async_copy(seen, seen, line_recv.at[sweep]).wait()
        row_totals = line_in[sweep, 0]
        for layer in range(1, N_Z):
            row_totals += line_in[sweep, layer]
        parts = split(row_totals)
        by_slot = jnp.zeros((LAYER, LAYER * CAP), F32)
        for layer in range(N_Z):
            product = lax.dot_general(
                parts, picks[layer], (((1,), (1,)), ((), ())), preferred_element_type=F32
            )
            by_slot += own_row(product, layer)
        for j in range(N_X):
            total[sweep, j] = by_slot[:N_Z, 128 * j : 128 * (j + 1)]
        exchange_seats(total, total_in, sweep, total_send, total_recv)
        totals = take_halves(total_in, sweep)
        live = totals > 0.0
        inverse = jnp.where(live, 1.0 / jnp.where(live, totals, 1.0), 0.0)

        mass_part = jnp.zeros((BLOCK, 128), F32)
        for layer in range(N_Z):
            for j in range(N_X):
                start = layer * LAYER * CAP + 128 * j
                piece = slice(start, start + 128)
                shares = raw[:, piece] * inverse[layer : layer + 1, 128 * j : 128 * (j + 1)]
                low[:, piece] = shares.astype(BF16)
                mass_part += shares
        mass_row = jnp.sum(jnp.transpose(mass_part), axis=0, keepdims=True)
        for h in range(2):
            edge_out[h, 1:2, :] = mass_row[:, half * h : half * (h + 1)]

        def sum_step(i, inner):
            far_z = lax.rem(dp // N_Y + 1 - lax.rem(i, 2), 2)
            far_y = lax.rem(dp // 4 + 1 - i // 2, 2)
            j = far_z * 2 + far_y
            block_rows = rows[:, :, lanes(j * 256, 256)].reshape(SLOTS, 256)
            sums = jnp.dot(low[...], block_rows, preferred_element_type=F32)
            for h in range(2):
                for k in range(2):
                    top = sums[half * h : half * h + quarter, 128 * k : 128 * (k + 1)]
                    bottom = sums[half * h + quarter : half * (h + 1), 128 * k : 128 * (k + 1)]
                    even = jnp.where(left, top, pltpu.roll(bottom, 64, 1))
                    odd = jnp.where(left, pltpu.roll(top, 64, 1), bottom)
                    panel_out[sweep, h, 4 * j + 2 * k] = even.astype(BF16)
                    panel_out[sweep, h, 4 * j + 2 * k + 1] = odd.astype(BF16)
            for k in range(4):
                target = 4 * j + lax.rem(dp + 2 + k, 4)

                @pl.when(target != dp)
                def _():
                    panel_copy(sweep, 0, target).start()

            return inner

        lax.fori_loop(0, N_DP // 4, sum_step, 0)

        def send_second(i, inner):
            panel_copy(sweep, 1, dp_peer(i)).start()
            return inner

        lax.fori_loop(0, N_DP - 1, send_second, 0)

        for h in range(2):
            panel_in[sweep, h, dp] = panel_out[sweep, h, dp]
            seen = panel_in.at[sweep, h, pl.ds(0, N_DP - 1)]
            pltpu.make_async_copy(seen, seen, panel_recv.at[sweep, h]).wait()
            sums_panel = panel_in[sweep, h, 0].astype(F32)
            for j in range(1, N_DP):
                sums_panel += panel_in[sweep, h, j].astype(F32)

            @pl.when(sweep < ITERS - 1)
            def _():
                fresh[sweep + 1, h, dp] = sums_panel.astype(BF16)

                def send_fresh(i, inner):
                    fresh_copy(sweep + 1, h, i).start()
                    return inner

                lax.fori_loop(0, N_DP - 1, send_fresh, 0)

            @pl.when(sweep == ITERS - 1)
            def _():
                along = jnp.transpose(jnp.concatenate([sums_panel, sums_panel], axis=0))
                across = jnp.where(left, along[:PANEL], along[PANEL:])
                last_sums[h] = across
                edge_out[h, 0:1, :] = jnp.sum(across * across, axis=0, keepdims=True)

                def send_edge(i, inner):
                    edge_copy(h, i).start()
                    return inner

                lax.fori_loop(0, N_DP - 1, send_edge, 0)
                edge_in[h, dp] = edge_out[h]

        return carry

    lax.fori_loop(0, ITERS, sweep_step, 0)

    for h in range(2):
        seen = edge_in.at[h, pl.ds(0, N_DP - 1)]
        pltpu.make_async_copy(seen, seen, edge_recv.at[h]).wait()
        edges = edge_in[h, 0]
        for j in range(1, N_DP):
            edges += edge_in[h, j]
        scales = lax.rsqrt(edges[0:1] / D + EPSILON)
        out_ref[:, half * h : half * (h + 1)] = last_sums[h] * scales
        mass_ref[:, half * h : half * (h + 1)] = edges[1:2]

    def leave(sweep, carry):
        for ref, sem, count in (
            (part_in, part_send, LAYER - 1),
            (line_in, line_send, N_Z - 1),
            (total_in, total_send, LAYER - 1),
        ):
            sent = ref.at[sweep, pl.ds(0, count)]
            pltpu.make_async_copy(sent, sent, sem.at[sweep]).wait()
        for h in range(2):
            sent = panel_in.at[sweep, h, pl.ds(0, N_DP - 1)]
            pltpu.make_async_copy(sent, sent, panel_send.at[sweep, h]).wait()
        return carry

    lax.fori_loop(0, ITERS, leave, 0)
    for h in range(2):
        sent = fresh.at[1, h, pl.ds(0, N_DP - 1)]
        pltpu.make_async_copy(sent, sent, fresh_send.at[h]).wait()
        sent = edge_in.at[h, pl.ds(0, N_DP - 1)]
        pltpu.make_async_copy(sent, sent, edge_send.at[h]).wait()
    pair_copy.wait_send()
    sent = fresh.at[0, :, pl.ds(0, 2 * (N_Y - 1))]
    pltpu.make_async_copy(sent, sent, first_sems.at[0]).wait()

    def leave_origin(origin, carry):
        def step(i, inner):
            row_copy(origin, i).wait_send()
            return inner

        lax.fori_loop(0, LAYER - 1, step, 0)

        @pl.when(jnp.logical_and(origin <= z, z < N_Z - 1))
        def _():
            unit_copy(origin, 1).wait_send()

        @pl.when(jnp.logical_and(origin >= z, z > 0))
        def _():
            unit_copy(origin, 0).wait_send()

        @pl.when(origin != z)
        def _():
            rank_copy(origin).wait_send()

        return carry

    lax.fori_loop(0, N_Z, leave_origin, 0)


def body(vectors, candidates, centroids):
    vmem = pl.BlockSpec(memory_space=pltpu.VMEM)
    dma = pltpu.SemaphoreType.DMA
    panel, mass = pl.pallas_call(
        kernel,
        out_shape=(
            jax.ShapeDtypeStruct((PANEL, BLOCK), F32),
            jax.ShapeDtypeStruct((1, BLOCK), F32),
        ),
        in_specs=[pl.BlockSpec(memory_space=pltpu.HBM)] * 3,
        out_specs=(vmem, vmem),
        scratch_shapes=[
            pltpu.VMEM((ROWS, D), BF16),
            pltpu.VMEM(candidates.shape[::-1], jnp.int32),
            pltpu.VMEM((PANEL, BLOCK), BF16),
            dma((3,)),
            pltpu.VMEM((N_Z, ROWS, D), BF16),
            pltpu.VMEM((N_Z, 2, LAYER, ROWS), jnp.int32),
            pltpu.VMEM((N_Z, LAYER * CAP, ROWS), BF16),
            pltpu.VMEM((N_Z, LAYER, CAP, D), BF16),
            pltpu.VMEM((N_CENT, CAP, D), BF16),
            pltpu.VMEM((BLOCK, SLOTS), F32),
            pltpu.VMEM((BLOCK, SLOTS), BF16),
            pltpu.VMEM((ITERS, N_X, N_Z, 128), F32),
            pltpu.VMEM((ITERS, LAYER, N_Z, 128), F32),
            pltpu.VMEM((ITERS, N_Z, N_Z, ROWS), F32),
            pltpu.VMEM((ITERS, N_X, N_Z, 128), F32),
            pltpu.VMEM((ITERS, LAYER, N_Z, 128), F32),
            pltpu.VMEM((BLOCK // 2, D), F32),
            pltpu.VMEM((BLOCK, D), BF16),
            pltpu.VMEM((ITERS, 2, N_DP, BLOCK // 4, 128), BF16),
            pltpu.VMEM((ITERS, 2, N_DP, BLOCK // 4, 128), BF16),
            pltpu.VMEM((ITERS, 2, N_DP, BLOCK // 4, 128), BF16),
            pltpu.VMEM((2, PANEL, 128), F32),
            pltpu.VMEM((2, 2, 128), F32),
            pltpu.VMEM((2, N_DP, 2, 128), F32),
            pltpu.SemaphoreType.REGULAR,
            dma((N_Z, 2)),
            dma((N_Z,)),
            dma((N_Z,)),
            dma((N_Z,)),
            dma((N_Z, LAYER)),
            dma((N_CENT,)),
            dma((2,)),
            dma((2,)),
            dma((ITERS,)),
            dma((ITERS,)),
            dma((ITERS,)),
            dma((ITERS,)),
            dma((ITERS,)),
            dma((ITERS,)),
            dma((ITERS, 2)),
            dma((ITERS, 2)),
            dma((2,)),
            dma((2,)),
            dma((2,)),
            dma((2,)),
        ],
        compiler_params=pltpu.CompilerParams(
            collective_id=0, has_side_effects=True, vmem_limit_bytes=60 * 1024 * 1024
        ),
        cost_estimate=pl.CostEstimate(
            flops=9 * 2 * SLOTS * BLOCK * D // 2, bytes_accessed=4 << 20, transcendentals=SLOTS * BLOCK
        ),
        name="soft_kmeans",
    )(vectors, candidates.T, centroids.T)
    return panel.T, mass.reshape(BLOCK)


def solution(mesh):
    return jax.shard_map(
        body,
        mesh=mesh,
        in_specs=(P(("dp", "cent"), None), P(("dp", "cent"), None), P("cent", "dp")),
        out_specs=(P("cent", "dp"), P("cent")),
        check_vma=False,
    )
```

```python
import functools

import jax
import jax.numpy as jnp
from jax import lax
from jax.experimental import pallas as pl
from jax.experimental.pallas import tpu as pltpu
from jax.sharding import PartitionSpec as P

ITERS = 2
EPSILON = 1e-06
SHARPNESS = 20.0

D = 1024
ROWS = 256
BLOCK = 256
CAP = 64
N_DP = 16
N_CENT = 32
N_X = 4
N_Y = 8
N_Z = 4
LAYER = 8
SLOTS = N_CENT * CAP
PANEL = D // N_DP

F32 = jnp.float32
BF16 = jnp.bfloat16
MESH = pl.DeviceIdType.MESH


def lanes(start, size):
    return pl.ds(pl.multiple_of(start, 128), size)


def kernel(
    vec_hbm,
    cand_hbm,
    cent_hbm,
    out_ref,
    mass_ref,
    vec_ref,
    cand_ref,
    cent_ref,
    fetch_sems,
    units,
    ranks,
    picks,
    packed,
    rows,
    raw,
    low,
    part,
    part_in,
    line_in,
    total,
    total_in,
    wide,
    unit_cent,
    panel_out,
    panel_in,
    fresh,
    last_sums,
    edge_out,
    edge_in,
    vouched,
    z_send,
    z_recv,
    rank_send,
    rank_recv,
    x_send,
    x_recv,
    pair_sems,
    first_sems,
    part_send,
    part_recv,
    line_send,
    line_recv,
    total_send,
    total_recv,
    panel_send,
    panel_recv,
    fresh_send,
    fresh_recv,
    edge_send,
    edge_recv,
):
    dp = lax.axis_index("dp")
    cent = lax.axis_index("cent")
    x = cent // LAYER
    z = (cent // 2) % N_Z
    core = cent % 2
    seat = x * 2 + core

    def offset(i):
        return 4 + i // 2 - lax.rem(i, 2) * (2 * (i // 2) + 1)

    def dp_peer(i):
        z_of = lax.rem(dp // N_Y + 1 - lax.rem(i, 2), 2)
        return z_of * N_Y + lax.rem(dp + offset(i // 2), N_Y)

    def y_peer(i):
        return (dp // N_Y) * N_Y + lax.rem(dp + offset(i), N_Y)

    other_dp = lax.rem(dp + N_Y, N_DP)

    def seat_peer(i):
        return lax.rem(seat + offset(i), LAYER)

    def z_peer(i):
        return lax.rem(z + i, N_Z)

    def at_seat(other):
        return (dp, (other // 2) * LAYER + z * 2 + other % 2)

    def at_layer(other):
        return (dp, x * LAYER + other * 2 + core)

    barrier = pltpu.get_barrier_semaphore()

    def greet_seat(i, carry):
        pl.semaphore_signal(barrier, inc=1, device_id=at_seat(seat_peer(i)), device_id_type=MESH)
        return carry

    def greet_layer(i, carry):
        pl.semaphore_signal(barrier, inc=1, device_id=at_layer(z_peer(i)), device_id_type=MESH)
        return carry

    def greet_y(i, carry):
        pl.semaphore_signal(barrier, inc=1, device_id=(y_peer(i), cent), device_id_type=MESH)
        return carry

    lax.fori_loop(0, LAYER - 1, greet_seat, 0)
    lax.fori_loop(1, N_Z, greet_layer, 0)
    lax.fori_loop(0, N_Y - 1, greet_y, 0)
    pl.semaphore_signal(barrier, inc=1, device_id=(other_dp, cent), device_id_type=MESH)

    fetches = [
        pltpu.make_async_copy(source, place, sem)
        for source, place, sem in (
            (vec_hbm, vec_ref, fetch_sems.at[0]),
            (cand_hbm, cand_ref, fetch_sems.at[1]),
            (cent_hbm, cent_ref, fetch_sems.at[2]),
        )
    ]
    for fetch in fetches:
        fetch.start()
    for fetch in fetches:
        fetch.wait()

    vec = vec_ref[...].astype(F32)
    vec_scale = lax.rsqrt(jnp.mean(vec * vec, axis=1, keepdims=True) + EPSILON)
    units[z] = (vec * vec_scale).astype(BF16)
    cand = cand_ref[...]
    place = lax.broadcasted_iota(jnp.int32, (N_CENT, ROWS), 0)
    block = ((place >> 1) & (N_X - 1)) * LAYER + (place >> 3) * 2 + (place & 1)
    named = cand[0:1, :] == block
    for j in range(1, cand.shape[0]):
        named = jnp.logical_or(named, cand[j : j + 1, :] == block)
    named_f = jnp.where(named, 1.0, 0.0)
    first = lax.broadcasted_iota(jnp.int32, (ROWS, ROWS), 0)
    second = lax.broadcasted_iota(jnp.int32, (ROWS, ROWS), 1)
    before = jnp.where(first < second, 1.0, 0.0).astype(BF16)
    rank = jnp.dot(named_f.astype(BF16), before, preferred_element_type=F32)
    slots = jnp.where(named, rank, -1.0).astype(jnp.int32)
    for layer in range(N_Z):
        ranks[layer, 0] = slots[layer * LAYER : (layer + 1) * LAYER]

    slot_iota = lax.broadcasted_iota(jnp.int32, (CAP, ROWS), 0)

    def pick_rows(rank_rows):
        picks = [
            jnp.where(rank_rows[j : j + 1, :] == slot_iota, 1.0, 0.0).astype(BF16)
            for j in range(LAYER)
        ]
        return jnp.concatenate(picks, axis=0)

    def pack(origin, rank_rows):
        picks[origin] = pick_rows(rank_rows)
        chosen = jnp.dot(picks[origin], units[origin], preferred_element_type=F32)
        packed[origin] = chosen.astype(BF16).reshape(LAYER, CAP, D)
        rows[origin * LAYER + seat] = packed[origin, seat]

    half = BLOCK // 2
    quarter = half // 2
    left = lax.broadcasted_iota(jnp.int32, (quarter, 128), 1) < PANEL
    for h in range(2):
        across = cent_ref[:, half * h : half * (h + 1)].astype(F32)
        along = jnp.transpose(jnp.concatenate([across, across], axis=0))
        fresh[0, h, dp] = jnp.where(left, along[:quarter], along[quarter:]).astype(BF16)

    pack(z, ranks[z, 0])

    pl.semaphore_wait(barrier, LAYER - 1 + N_Z - 1 + N_Y)
    pl.semaphore_signal(vouched, inc=1, device_id=(other_dp, cent), device_id_type=MESH)

    pair_copy = pltpu.make_async_remote_copy(
        src_ref=fresh.at[0, :, dp],
        dst_ref=fresh.at[0, :, dp],
        send_sem=pair_sems.at[0],
        recv_sem=pair_sems.at[1],
        device_id=(other_dp, cent),
        device_id_type=MESH,
    )
    pair_copy.start()

    def rank_copy(layer):
        return pltpu.make_async_remote_copy(
            src_ref=ranks.at[layer, 0],
            dst_ref=ranks.at[z, 1],
            send_sem=rank_send.at[layer],
            recv_sem=rank_recv.at[z],
            device_id=at_layer(layer),
            device_id_type=MESH,
        )

    def unit_copy(origin, side):
        return pltpu.make_async_remote_copy(
            src_ref=units.at[origin],
            dst_ref=units.at[origin],
            send_sem=z_send.at[origin, side],
            recv_sem=z_recv.at[origin],
            device_id=at_layer(z + 2 * side - 1),
            device_id_type=MESH,
        )

    def start_up(origin):
        @pl.when(z < N_Z - 1)
        def _():
            unit_copy(origin, 1).start()

    def start_down(origin):
        @pl.when(z > 0)
        def _():
            unit_copy(origin, 0).start()

    start_up(z)
    start_down(z)

    def send_rank(i, carry):
        rank_copy(z_peer(i)).start()
        return carry

    lax.fori_loop(1, N_Z, send_rank, 0)


    def first_copy(which, i):
        return pltpu.make_async_remote_copy(
            src_ref=fresh.at[0, :, which],
            dst_ref=fresh.at[0, :, which],
            send_sem=first_sems.at[0],
            recv_sem=first_sems.at[1],
            device_id=(y_peer(i), cent),
            device_id_type=MESH,
        )

    def fresh_copy(sweep, h, i):
        return pltpu.make_async_remote_copy(
            src_ref=fresh.at[sweep, h, dp],
            dst_ref=fresh.at[sweep, h, dp],
            send_sem=fresh_send.at[h],
            recv_sem=fresh_recv.at[h],
            device_id=(dp_peer(i), cent),
            device_id_type=MESH,
        )

    def row_copy(origin, i):
        target = seat_peer(i)
        return pltpu.make_async_remote_copy(
            src_ref=packed.at[origin, target],
            dst_ref=rows.at[origin * LAYER + seat],
            send_sem=x_send.at[origin, target],
            recv_sem=x_recv.at[origin * LAYER + seat],
            device_id=at_seat(target),
            device_id_type=MESH,
        )

    def send_packed(origin):
        def step(i, carry):
            row_copy(origin, i).start()
            return carry

        lax.fori_loop(0, LAYER - 1, step, 0)

    send_packed(z)

    def event(e, carry):
        distance = (e + 1) // 2
        up = lax.rem(e, 2)
        origin = z + jnp.where(up == 1, -distance, distance)

        @pl.when(jnp.logical_and(origin >= 0, origin < N_Z))
        def _():
            unit_copy(origin, 0).wait_recv()

            @pl.when(up == 1)
            def _():
                start_up(origin)

            @pl.when(up == 0)
            def _():
                start_down(origin)

            rank_copy_in(origin).wait_recv()

        return carry

    def pack_event(e, carry):
        distance = (e + 1) // 2
        up = lax.rem(e, 2)
        origin = z + jnp.where(up == 1, -distance, distance)

        @pl.when(jnp.logical_and(origin >= 0, origin < N_Z))
        def _():
            pack(origin, ranks[origin, 1])
            send_packed(origin)

        return carry

    def rank_copy_in(origin):
        return pltpu.make_async_remote_copy(
            src_ref=ranks.at[origin, 0],
            dst_ref=ranks.at[origin, 1],
            send_sem=rank_send.at[origin],
            recv_sem=rank_recv.at[origin],
            device_id=at_layer(origin),
            device_id_type=MESH,
        )

    lax.fori_loop(1, 3, event, 0)
    lax.fori_loop(1, 3, pack_event, 0)
    pair_copy.wait_recv()

    def send_first(i, carry):
        first_copy(dp, i).start()
        first_copy(other_dp, i).start()
        return carry

    lax.fori_loop(0, N_Y - 1, send_first, 0)
    lax.fori_loop(3, 5, event, 0)
    lax.fori_loop(3, 5, pack_event, 0)
    lax.fori_loop(5, 7, event, 0)
    lax.fori_loop(5, 7, pack_event, 0)
    pl.semaphore_wait(vouched, 1)

    left_four = lax.broadcasted_iota(jnp.int32, (N_Z, 128), 1) < CAP
    layer_iota = lax.broadcasted_iota(jnp.int32, (LAYER, 1), 0)

    def take_halves(ref, sweep):
        pieces = []
        for j in range(LAYER // 2):
            even = ref[sweep, 2 * j]
            odd = ref[sweep, 2 * j + 1]
            first_core = jnp.where(left_four, even, pltpu.roll(odd, 64, 1))
            second_core = jnp.where(left_four, pltpu.roll(even, 64, 1), odd)
            pieces.append(jnp.where(core == 0, first_core, second_core))
        return jnp.concatenate(pieces, axis=1)

    def split(four):
        zeros = jnp.zeros((LAYER - N_Z, four.shape[1]), F32)
        value = jnp.concatenate([four, zeros], axis=0)
        high = value.astype(BF16).astype(F32)
        rest = value - high
        middle = rest.astype(BF16).astype(F32)
        return jnp.concatenate([high, middle, rest - middle], axis=0).astype(BF16)

    def own_row(product, layer):
        added = product[:LAYER] + product[LAYER : 2 * LAYER] + product[2 * LAYER :]
        return jnp.where(layer_iota == layer, added, 0.0)

    def seat_copy(source, target, sweep, i, send_sem, recv_sem):
        other = seat_peer(i)
        return pltpu.make_async_remote_copy(
            src_ref=source.at[sweep, other // 2],
            dst_ref=target.at[sweep, seat],
            send_sem=send_sem.at[sweep],
            recv_sem=recv_sem.at[sweep],
            device_id=at_seat(other),
            device_id_type=MESH,
        )

    def exchange_seats(source, target, sweep, send_sem, recv_sem):
        def step(i, carry):
            seat_copy(source, target, sweep, i, send_sem, recv_sem).start()
            return carry

        lax.fori_loop(0, LAYER - 1, step, 0)
        target[sweep, seat] = source[sweep, x]
        seen = target.at[sweep, pl.ds(0, LAYER - 1)]
        pltpu.make_async_copy(seen, seen, recv_sem.at[sweep]).wait()

    def line_copy(sweep, i):
        return pltpu.make_async_remote_copy(
            src_ref=line_in.at[sweep, z],
            dst_ref=line_in.at[sweep, z],
            send_sem=line_send.at[sweep],
            recv_sem=line_recv.at[sweep],
            device_id=at_layer(z_peer(i)),
            device_id_type=MESH,
        )

    def edge_copy(h, i):
        return pltpu.make_async_remote_copy(
            src_ref=edge_out.at[h],
            dst_ref=edge_in.at[h, dp],
            send_sem=edge_send.at[h],
            recv_sem=edge_recv.at[h],
            device_id=(dp_peer(i), cent),
            device_id_type=MESH,
        )

    def panel_copy(sweep, h, target):
        return pltpu.make_async_remote_copy(
            src_ref=panel_out.at[sweep, h, target],
            dst_ref=panel_in.at[sweep, h, dp],
            send_sem=panel_send.at[sweep, h],
            recv_sem=panel_recv.at[sweep, h],
            device_id=(target, cent),
            device_id_type=MESH,
        )

    def unit_scale(squares, sweep):
        mean = jnp.sum(squares, axis=1, keepdims=True) / D
        scale = jnp.where(sweep == 0, 1.0, lax.rsqrt(mean + EPSILON))
        return scale * lax.rsqrt(mean * scale * scale + EPSILON)

    def leave_origin(origin, carry):
        def step(i, inner):
            row_copy(origin, i).wait_send()
            return inner

        lax.fori_loop(0, LAYER - 1, step, 0)

        @pl.when(jnp.logical_and(origin <= z, z < N_Z - 1))
        def _():
            unit_copy(origin, 1).wait_send()

        @pl.when(jnp.logical_and(origin >= z, z > 0))
        def _():
            unit_copy(origin, 0).wait_send()

        @pl.when(origin != z)
        def _():
            rank_copy(origin).wait_send()

        return carry

    def sweep_step(sweep, carry):
        def unit_half(h):
            low_row, high_row = half * h, half * h + quarter
            top_squares = jnp.zeros((quarter, 128), F32)
            bottom_squares = jnp.zeros((quarter, 128), F32)
            for j in range(N_DP // 2):
                even = fresh[sweep, h, 2 * j].astype(F32)
                odd = fresh[sweep, h, 2 * j + 1].astype(F32)
                top = jnp.where(left, even, pltpu.roll(odd, 64, 1))
                bottom = jnp.where(left, pltpu.roll(even, 64, 1), odd)
                wide[:quarter, 128 * j : 128 * (j + 1)] = top
                wide[quarter:, 128 * j : 128 * (j + 1)] = bottom
                top_squares += top * top
                bottom_squares += bottom * bottom
            top_scale = unit_scale(top_squares, sweep)
            bottom_scale = unit_scale(bottom_squares, sweep)
            unit_cent[low_row:high_row] = (wide[:quarter] * top_scale).astype(BF16)
            unit_cent[high_row : half * (h + 1)] = (wide[quarter:] * bottom_scale).astype(BF16)

        def score(origin, start, size):
            mine = rows[pl.ds(origin * LAYER, LAYER)].reshape(LAYER * CAP, D)
            scores = lax.dot_general(
                unit_cent[start : start + size],
                mine,
                (((1,), (1,)), ((), ())),
                preferred_element_type=F32,
            )
            weights = jnp.exp(scores * (SHARPNESS / D))
            raw[start : start + size, lanes(origin * LAYER * CAP, LAYER * CAP)] = weights
            added = jnp.sum(weights, axis=0, keepdims=True)
            for j in range(N_X):
                piece = added[:, 128 * j : 128 * (j + 1)]
                if start > 0:
                    piece += part[sweep, j, pl.ds(origin, 1), :]
                part[sweep, j, pl.ds(origin, 1), :] = piece

        @pl.when(sweep == 0)
        def _():
            seen = fresh.at[0, :, pl.ds(0, 2 * (N_Y - 1))]
            pltpu.make_async_copy(seen, seen, first_sems.at[1]).wait()
            for h in range(2):
                unit_half(h)

            def score_arrived(g, inner):
                distance = (g + 1) // 2
                origin = z + jnp.where(lax.rem(g, 2) == 1, -distance, distance)

                @pl.when(jnp.logical_and(origin >= 0, origin < N_Z))
                def _():
                    def arrive(i, deep):
                        sender = seat_peer(i)
                        slot = rows.at[origin * LAYER + sender]
                        pltpu.make_async_copy(
                            slot, slot, x_recv.at[origin * LAYER + sender]
                        ).wait()
                        return deep

                    lax.fori_loop(0, LAYER - 1, arrive, 0)
                    score(origin, 0, BLOCK)

                return inner

            lax.fori_loop(0, 2 * N_Z - 1, score_arrived, 0)

        @pl.when(sweep > 0)
        def _():
            for h in range(2):
                seen = fresh.at[sweep, h, pl.ds(0, N_DP - 1)]
                pltpu.make_async_copy(seen, seen, fresh_recv.at[h]).wait()
                unit_half(h)

                def score_half(origin, inner):
                    score(origin, half * h, half)
                    return inner

                lax.fori_loop(0, N_Z, score_half, 0)

        exchange_seats(part, part_in, sweep, part_send, part_recv)
        parts = split(take_halves(part_in, sweep))
        by_row = jnp.zeros((LAYER, ROWS), F32)
        for layer in range(N_Z):
            product = jnp.dot(parts, picks[layer], preferred_element_type=F32)
            by_row += own_row(product, layer)
        line_in[sweep, z] = by_row[:N_Z]

        def send_line(i, inner):
            line_copy(sweep, i).start()
            return inner

        lax.fori_loop(1, N_Z, send_line, 0)
        seen = line_in.at[sweep, pl.ds(0, N_Z - 1)]
        pltpu.make_async_copy(seen, seen, line_recv.at[sweep]).wait()
        row_totals = line_in[sweep, 0]
        for layer in range(1, N_Z):
            row_totals += line_in[sweep, layer]
        parts = split(row_totals)
        by_slot = jnp.zeros((LAYER, LAYER * CAP), F32)
        for layer in range(N_Z):
            product = lax.dot_general(
                parts, picks[layer], (((1,), (1,)), ((), ())), preferred_element_type=F32
            )
            by_slot += own_row(product, layer)
        for j in range(N_X):
            total[sweep, j] = by_slot[:N_Z, 128 * j : 128 * (j + 1)]
        exchange_seats(total, total_in, sweep, total_send, total_recv)
        totals = take_halves(total_in, sweep)
        live = totals > 0.0
        inverse = jnp.where(live, 1.0 / jnp.where(live, totals, 1.0), 0.0)

        mass_part = jnp.zeros((BLOCK, 128), F32)
        for layer in range(N_Z):
            for j in range(N_X):
                start = layer * LAYER * CAP + 128 * j
                piece = slice(start, start + 128)
                shares = raw[:, piece] * inverse[layer : layer + 1, 128 * j : 128 * (j + 1)]
                low[:, piece] = shares.astype(BF16)
                mass_part += shares
        mass_row = jnp.sum(jnp.transpose(mass_part), axis=0, keepdims=True)
        for h in range(2):
            edge_out[h, 1:2, :] = mass_row[:, half * h : half * (h + 1)]

        def sum_step(i, inner):
            far_z = lax.rem(dp // N_Y + 1 - lax.rem(i, 2), 2)
            far_y = lax.rem(dp // 4 + 1 - i // 2, 2)
            j = far_z * 2 + far_y
            block_rows = rows[:, :, lanes(j * 256, 256)].reshape(SLOTS, 256)
            sums = jnp.dot(low[...], block_rows, preferred_element_type=F32)
            for h in range(2):
                for k in range(2):
                    top = sums[half * h : half * h + quarter, 128 * k : 128 * (k + 1)]
                    bottom = sums[half * h + quarter : half * (h + 1), 128 * k : 128 * (k + 1)]
                    even = jnp.where(left, top, pltpu.roll(bottom, 64, 1))
                    odd = jnp.where(left, pltpu.roll(top, 64, 1), bottom)
                    panel_out[sweep, h, 4 * j + 2 * k] = even.astype(BF16)
                    panel_out[sweep, h, 4 * j + 2 * k + 1] = odd.astype(BF16)
            for k in range(4):
                target = 4 * j + lax.rem(dp + 2 + k, 4)

                @pl.when(target != dp)
                def _():
                    panel_copy(sweep, 0, target).start()

            return inner

        lax.fori_loop(0, N_DP // 4, sum_step, 0)

        def send_second(i, inner):
            panel_copy(sweep, 1, dp_peer(i)).start()
            return inner

        lax.fori_loop(0, N_DP - 1, send_second, 0)

        for ref, sem, count in (
            (part_in, part_send, LAYER - 1),
            (line_in, line_send, N_Z - 1),
            (total_in, total_send, LAYER - 1),
        ):
            sent = ref.at[sweep, pl.ds(0, count)]
            pltpu.make_async_copy(sent, sent, sem.at[sweep]).wait()

        @pl.when(sweep == 0)
        def _():
            lax.fori_loop(0, N_Z, leave_origin, 0)

        for h in range(2):
            panel_in[sweep, h, dp] = panel_out[sweep, h, dp]
            seen = panel_in.at[sweep, h, pl.ds(0, N_DP - 1)]
            pltpu.make_async_copy(seen, seen, panel_recv.at[sweep, h]).wait()
            sums_panel = panel_in[sweep, h, 0].astype(F32)
            for j in range(1, N_DP):
                sums_panel += panel_in[sweep, h, j].astype(F32)

            @pl.when(sweep < ITERS - 1)
            def _():
                fresh[sweep + 1, h, dp] = sums_panel.astype(BF16)

                def send_fresh(i, inner):
                    fresh_copy(sweep + 1, h, i).start()
                    return inner

                lax.fori_loop(0, N_DP - 1, send_fresh, 0)

            @pl.when(sweep == ITERS - 1)
            def _():
                along = jnp.transpose(jnp.concatenate([sums_panel, sums_panel], axis=0))
                across = jnp.where(left, along[:PANEL], along[PANEL:])
                last_sums[h] = across
                edge_out[h, 0:1, :] = jnp.sum(across * across, axis=0, keepdims=True)

                def send_edge(i, inner):
                    edge_copy(h, i).start()
                    return inner

                lax.fori_loop(0, N_DP - 1, send_edge, 0)
                edge_in[h, dp] = edge_out[h]

        return carry

    lax.fori_loop(0, ITERS, sweep_step, 0)

    for h in range(2):
        seen = edge_in.at[h, pl.ds(0, N_DP - 1)]
        pltpu.make_async_copy(seen, seen, edge_recv.at[h]).wait()
        edges = edge_in[h, 0]
        for j in range(1, N_DP):
            edges += edge_in[h, j]
        scales = lax.rsqrt(edges[0:1] / D + EPSILON)
        out_ref[:, half * h : half * (h + 1)] = last_sums[h] * scales
        mass_ref[:, half * h : half * (h + 1)] = edges[1:2]

    for sweep in range(ITERS):
        for h in range(2):
            sent = panel_in.at[sweep, h, pl.ds(0, N_DP - 1)]
            pltpu.make_async_copy(sent, sent, panel_send.at[sweep, h]).wait()
    for h in range(2):
        sent = fresh.at[1, h, pl.ds(0, N_DP - 1)]
        pltpu.make_async_copy(sent, sent, fresh_send.at[h]).wait()
        sent = edge_in.at[h, pl.ds(0, N_DP - 1)]
        pltpu.make_async_copy(sent, sent, edge_send.at[h]).wait()
    pair_copy.wait_send()
    sent = fresh.at[0, :, pl.ds(0, 2 * (N_Y - 1))]
    pltpu.make_async_copy(sent, sent, first_sems.at[0]).wait()


def body(vectors, candidates, centroids):
    vmem = pl.BlockSpec(memory_space=pltpu.VMEM)
    dma = pltpu.SemaphoreType.DMA
    panel, mass = pl.pallas_call(
        kernel,
        out_shape=(
            jax.ShapeDtypeStruct((PANEL, BLOCK), F32),
            jax.ShapeDtypeStruct((1, BLOCK), F32),
        ),
        in_specs=[pl.BlockSpec(memory_space=pltpu.HBM)] * 3,
        out_specs=(vmem, vmem),
        scratch_shapes=[
            pltpu.VMEM((ROWS, D), BF16),
            pltpu.VMEM(candidates.shape[::-1], jnp.int32),
            pltpu.VMEM((PANEL, BLOCK), BF16),
            dma((3,)),
            pltpu.VMEM((N_Z, ROWS, D), BF16),
            pltpu.VMEM((N_Z, 2, LAYER, ROWS), jnp.int32),
            pltpu.VMEM((N_Z, LAYER * CAP, ROWS), BF16),
            pltpu.VMEM((N_Z, LAYER, CAP, D), BF16),
            pltpu.VMEM((N_CENT, CAP, D), BF16),
            pltpu.VMEM((BLOCK, SLOTS), F32),
            pltpu.VMEM((BLOCK, SLOTS), BF16),
            pltpu.VMEM((ITERS, N_X, N_Z, 128), F32),
            pltpu.VMEM((ITERS, LAYER, N_Z, 128), F32),
            pltpu.VMEM((ITERS, N_Z, N_Z, ROWS), F32),
            pltpu.VMEM((ITERS, N_X, N_Z, 128), F32),
            pltpu.VMEM((ITERS, LAYER, N_Z, 128), F32),
            pltpu.VMEM((BLOCK // 2, D), F32),
            pltpu.VMEM((BLOCK, D), BF16),
            pltpu.VMEM((ITERS, 2, N_DP, BLOCK // 4, 128), BF16),
            pltpu.VMEM((ITERS, 2, N_DP, BLOCK // 4, 128), BF16),
            pltpu.VMEM((ITERS, 2, N_DP, BLOCK // 4, 128), BF16),
            pltpu.VMEM((2, PANEL, 128), F32),
            pltpu.VMEM((2, 2, 128), F32),
            pltpu.VMEM((2, N_DP, 2, 128), F32),
            pltpu.SemaphoreType.REGULAR,
            dma((N_Z, 2)),
            dma((N_Z,)),
            dma((N_Z,)),
            dma((N_Z,)),
            dma((N_Z, LAYER)),
            dma((N_CENT,)),
            dma((2,)),
            dma((2,)),
            dma((ITERS,)),
            dma((ITERS,)),
            dma((ITERS,)),
            dma((ITERS,)),
            dma((ITERS,)),
            dma((ITERS,)),
            dma((ITERS, 2)),
            dma((ITERS, 2)),
            dma((2,)),
            dma((2,)),
            dma((2,)),
            dma((2,)),
        ],
        compiler_params=pltpu.CompilerParams(
            collective_id=0, has_side_effects=True, vmem_limit_bytes=60 * 1024 * 1024
        ),
        cost_estimate=pl.CostEstimate(
            flops=9 * 2 * SLOTS * BLOCK * D // 2, bytes_accessed=4 << 20, transcendentals=SLOTS * BLOCK
        ),
        name="soft_kmeans",
    )(vectors, candidates.T, centroids.T)
    return panel.T, mass.reshape(BLOCK)


def solution(mesh):
    return jax.shard_map(
        body,
        mesh=mesh,
        in_specs=(P(("dp", "cent"), None), P(("dp", "cent"), None), P("cent", "dp")),
        out_specs=(P("cent", "dp"), P("cent")),
        check_vma=False,
    )
```

```python
import functools

import jax
import jax.numpy as jnp
from jax import lax
from jax.experimental import pallas as pl
from jax.experimental.pallas import tpu as pltpu
from jax.sharding import PartitionSpec as P

ITERS = 2
EPSILON = 1e-06
SHARPNESS = 20.0

D = 1024
ROWS = 256
BLOCK = 256
CAP = 64
N_DP = 16
N_CENT = 32
N_X = 4
N_Y = 8
N_Z = 4
LAYER = 8
SLOTS = N_CENT * CAP
PANEL = D // N_DP

F32 = jnp.float32
BF16 = jnp.bfloat16
MESH = pl.DeviceIdType.MESH


def lanes(start, size):
    return pl.ds(pl.multiple_of(start, 128), size)


def kernel(
    vec_hbm,
    cand_hbm,
    cent_hbm,
    out_ref,
    mass_ref,
    vec_ref,
    cand_ref,
    cent_ref,
    fetch_sems,
    units,
    ranks,
    picks,
    packed,
    rows,
    raw,
    low,
    part,
    part_in,
    line_in,
    total,
    total_in,
    wide,
    unit_cent,
    panel_out,
    panel_in,
    fresh,
    last_sums,
    edge_out,
    edge_in,
    vouched,
    z_send,
    z_recv,
    rank_send,
    rank_recv,
    x_send,
    x_recv,
    pair_sems,
    first_sems,
    part_send,
    part_recv,
    line_send,
    line_recv,
    total_send,
    total_recv,
    panel_send,
    panel_recv,
    fresh_send,
    fresh_recv,
    edge_send,
    edge_recv,
):
    dp = lax.axis_index("dp")
    cent = lax.axis_index("cent")
    x = cent // LAYER
    z = (cent // 2) % N_Z
    core = cent % 2
    seat = x * 2 + core

    def offset(i):
        return 4 + i // 2 - lax.rem(i, 2) * (2 * (i // 2) + 1)

    def dp_peer(i):
        z_of = lax.rem(dp // N_Y + 1 - lax.rem(i, 2), 2)
        return z_of * N_Y + lax.rem(dp + offset(i // 2), N_Y)

    def y_peer(i):
        return (dp // N_Y) * N_Y + lax.rem(dp + offset(i), N_Y)

    other_dp = lax.rem(dp + N_Y, N_DP)

    def seat_peer(i):
        return lax.rem(seat + offset(i), LAYER)

    def z_peer(i):
        return lax.rem(z + i, N_Z)

    def at_seat(other):
        return (dp, (other // 2) * LAYER + z * 2 + other % 2)

    def at_layer(other):
        return (dp, x * LAYER + other * 2 + core)

    barrier = pltpu.get_barrier_semaphore()

    def greet_seat(i, carry):
        pl.semaphore_signal(barrier, inc=1, device_id=at_seat(seat_peer(i)), device_id_type=MESH)
        return carry

    def greet_layer(i, carry):
        pl.semaphore_signal(barrier, inc=1, device_id=at_layer(z_peer(i)), device_id_type=MESH)
        return carry

    def greet_y(i, carry):
        pl.semaphore_signal(barrier, inc=1, device_id=(y_peer(i), cent), device_id_type=MESH)
        return carry

    lax.fori_loop(0, LAYER - 1, greet_seat, 0)
    lax.fori_loop(1, N_Z, greet_layer, 0)
    lax.fori_loop(0, N_Y - 1, greet_y, 0)
    pl.semaphore_signal(barrier, inc=1, device_id=(other_dp, cent), device_id_type=MESH)

    fetches = [
        pltpu.make_async_copy(source, place, sem)
        for source, place, sem in (
            (vec_hbm, vec_ref, fetch_sems.at[0]),
            (cand_hbm, cand_ref, fetch_sems.at[1]),
            (cent_hbm, cent_ref, fetch_sems.at[2]),
        )
    ]
    for fetch in fetches:
        fetch.start()

    fetches[0].wait()
    vec = vec_ref[...].astype(F32)
    vec_scale = lax.rsqrt(jnp.mean(vec * vec, axis=1, keepdims=True) + EPSILON)
    units[z] = (vec * vec_scale).astype(BF16)

    pl.semaphore_wait(barrier, LAYER - 1 + N_Z - 1 + N_Y)
    pl.semaphore_signal(vouched, inc=1, device_id=(other_dp, cent), device_id_type=MESH)

    def unit_copy(origin, side):
        return pltpu.make_async_remote_copy(
            src_ref=units.at[origin],
            dst_ref=units.at[origin],
            send_sem=z_send.at[origin, side],
            recv_sem=z_recv.at[origin],
            device_id=at_layer(z + 2 * side - 1),
            device_id_type=MESH,
        )

    def start_up(origin):
        @pl.when(z < N_Z - 1)
        def _():
            unit_copy(origin, 1).start()

    def start_down(origin):
        @pl.when(z > 0)
        def _():
            unit_copy(origin, 0).start()

    start_up(z)
    start_down(z)

    fetches[1].wait()
    cand = cand_ref[...]
    place = lax.broadcasted_iota(jnp.int32, (N_CENT, ROWS), 0)
    block = ((place >> 1) & (N_X - 1)) * LAYER + (place >> 3) * 2 + (place & 1)
    named = cand[0:1, :] == block
    for j in range(1, cand.shape[0]):
        named = jnp.logical_or(named, cand[j : j + 1, :] == block)
    named_f = jnp.where(named, 1.0, 0.0)
    first = lax.broadcasted_iota(jnp.int32, (ROWS, ROWS), 0)
    second = lax.broadcasted_iota(jnp.int32, (ROWS, ROWS), 1)
    before = jnp.where(first < second, 1.0, 0.0).astype(BF16)
    rank = jnp.dot(named_f.astype(BF16), before, preferred_element_type=F32)
    slots = jnp.where(named, rank, -1.0).astype(jnp.int32)
    for layer in range(N_Z):
        ranks[layer, 0] = slots[layer * LAYER : (layer + 1) * LAYER]

    slot_iota = lax.broadcasted_iota(jnp.int32, (CAP, ROWS), 0)

    def pick_rows(rank_rows):
        picks = [
            jnp.where(rank_rows[j : j + 1, :] == slot_iota, 1.0, 0.0).astype(BF16)
            for j in range(LAYER)
        ]
        return jnp.concatenate(picks, axis=0)

    def pack(origin, rank_rows):
        picks[origin] = pick_rows(rank_rows)
        chosen = jnp.dot(picks[origin], units[origin], preferred_element_type=F32)
        packed[origin] = chosen.astype(BF16).reshape(LAYER, CAP, D)
        rows[origin * LAYER + seat] = packed[origin, seat]

    pack(z, ranks[z, 0])

    def rank_copy(layer):
        return pltpu.make_async_remote_copy(
            src_ref=ranks.at[layer, 0],
            dst_ref=ranks.at[z, 1],
            send_sem=rank_send.at[layer],
            recv_sem=rank_recv.at[z],
            device_id=at_layer(layer),
            device_id_type=MESH,
        )

    def send_rank(i, carry):
        rank_copy(z_peer(i)).start()
        return carry

    lax.fori_loop(1, N_Z, send_rank, 0)

    def first_copy(which, i):
        return pltpu.make_async_remote_copy(
            src_ref=fresh.at[0, :, which],
            dst_ref=fresh.at[0, :, which],
            send_sem=first_sems.at[0],
            recv_sem=first_sems.at[1],
            device_id=(y_peer(i), cent),
            device_id_type=MESH,
        )

    def fresh_copy(sweep, h, i):
        return pltpu.make_async_remote_copy(
            src_ref=fresh.at[sweep, h, dp],
            dst_ref=fresh.at[sweep, h, dp],
            send_sem=fresh_send.at[h],
            recv_sem=fresh_recv.at[h],
            device_id=(dp_peer(i), cent),
            device_id_type=MESH,
        )

    def row_copy(origin, i):
        target = seat_peer(i)
        return pltpu.make_async_remote_copy(
            src_ref=packed.at[origin, target],
            dst_ref=rows.at[origin * LAYER + seat],
            send_sem=x_send.at[origin, target],
            recv_sem=x_recv.at[origin * LAYER + seat],
            device_id=at_seat(target),
            device_id_type=MESH,
        )

    def send_packed(origin):
        def step(i, carry):
            row_copy(origin, i).start()
            return carry

        lax.fori_loop(0, LAYER - 1, step, 0)

    send_packed(z)

    fetches[2].wait()
    half = BLOCK // 2
    quarter = half // 2
    left = lax.broadcasted_iota(jnp.int32, (quarter, 128), 1) < PANEL
    for h in range(2):
        across = cent_ref[:, half * h : half * (h + 1)].astype(F32)
        along = jnp.transpose(jnp.concatenate([across, across], axis=0))
        fresh[0, h, dp] = jnp.where(left, along[:quarter], along[quarter:]).astype(BF16)

    pair_copy = pltpu.make_async_remote_copy(
        src_ref=fresh.at[0, :, dp],
        dst_ref=fresh.at[0, :, dp],
        send_sem=pair_sems.at[0],
        recv_sem=pair_sems.at[1],
        device_id=(other_dp, cent),
        device_id_type=MESH,
    )
    pair_copy.start()

    def event(e, carry):
        distance = (e + 1) // 2
        up = lax.rem(e, 2)
        origin = z + jnp.where(up == 1, -distance, distance)

        @pl.when(jnp.logical_and(origin >= 0, origin < N_Z))
        def _():
            unit_copy(origin, 0).wait_recv()

            @pl.when(up == 1)
            def _():
                start_up(origin)

            @pl.when(up == 0)
            def _():
                start_down(origin)

            rank_copy_in(origin).wait_recv()

        return carry

    def pack_event(e, carry):
        distance = (e + 1) // 2
        up = lax.rem(e, 2)
        origin = z + jnp.where(up == 1, -distance, distance)

        @pl.when(jnp.logical_and(origin >= 0, origin < N_Z))
        def _():
            pack(origin, ranks[origin, 1])
            send_packed(origin)

        return carry

    def rank_copy_in(origin):
        return pltpu.make_async_remote_copy(
            src_ref=ranks.at[origin, 0],
            dst_ref=ranks.at[origin, 1],
            send_sem=rank_send.at[origin],
            recv_sem=rank_recv.at[origin],
            device_id=at_layer(origin),
            device_id_type=MESH,
        )

    lax.fori_loop(1, 3, event, 0)
    lax.fori_loop(1, 3, pack_event, 0)
    pair_copy.wait_recv()

    def send_first(i, carry):
        first_copy(dp, i).start()
        first_copy(other_dp, i).start()
        return carry

    lax.fori_loop(0, N_Y - 1, send_first, 0)
    lax.fori_loop(3, 5, event, 0)
    lax.fori_loop(3, 5, pack_event, 0)
    lax.fori_loop(5, 7, event, 0)
    lax.fori_loop(5, 7, pack_event, 0)
    pl.semaphore_wait(vouched, 1)

    left_four = lax.broadcasted_iota(jnp.int32, (N_Z, 128), 1) < CAP
    layer_iota = lax.broadcasted_iota(jnp.int32, (LAYER, 1), 0)

    def take_halves(ref, sweep):
        pieces = []
        for j in range(LAYER // 2):
            even = ref[sweep, 2 * j]
            odd = ref[sweep, 2 * j + 1]
            first_core = jnp.where(left_four, even, pltpu.roll(odd, 64, 1))
            second_core = jnp.where(left_four, pltpu.roll(even, 64, 1), odd)
            pieces.append(jnp.where(core == 0, first_core, second_core))
        return jnp.concatenate(pieces, axis=1)

    def split(four):
        zeros = jnp.zeros((LAYER - N_Z, four.shape[1]), F32)
        value = jnp.concatenate([four, zeros], axis=0)
        high = value.astype(BF16).astype(F32)
        rest = value - high
        middle = rest.astype(BF16).astype(F32)
        return jnp.concatenate([high, middle, rest - middle], axis=0).astype(BF16)

    def own_row(product, layer):
        added = product[:LAYER] + product[LAYER : 2 * LAYER] + product[2 * LAYER :]
        return jnp.where(layer_iota == layer, added, 0.0)

    def seat_copy(source, target, sweep, i, send_sem, recv_sem):
        other = seat_peer(i)
        return pltpu.make_async_remote_copy(
            src_ref=source.at[sweep, other // 2],
            dst_ref=target.at[sweep, seat],
            send_sem=send_sem.at[sweep],
            recv_sem=recv_sem.at[sweep],
            device_id=at_seat(other),
            device_id_type=MESH,
        )

    def exchange_seats(source, target, sweep, send_sem, recv_sem):
        def step(i, carry):
            seat_copy(source, target, sweep, i, send_sem, recv_sem).start()
            return carry

        lax.fori_loop(0, LAYER - 1, step, 0)
        target[sweep, seat] = source[sweep, x]
        seen = target.at[sweep, pl.ds(0, LAYER - 1)]
        pltpu.make_async_copy(seen, seen, recv_sem.at[sweep]).wait()

    def line_copy(sweep, i):
        return pltpu.make_async_remote_copy(
            src_ref=line_in.at[sweep, z],
            dst_ref=line_in.at[sweep, z],
            send_sem=line_send.at[sweep],
            recv_sem=line_recv.at[sweep],
            device_id=at_layer(z_peer(i)),
            device_id_type=MESH,
        )

    def edge_copy(h, i):
        return pltpu.make_async_remote_copy(
            src_ref=edge_out.at[h],
            dst_ref=edge_in.at[h, dp],
            send_sem=edge_send.at[h],
            recv_sem=edge_recv.at[h],
            device_id=(dp_peer(i), cent),
            device_id_type=MESH,
        )

    def panel_copy(sweep, h, target):
        return pltpu.make_async_remote_copy(
            src_ref=panel_out.at[sweep, h, target],
            dst_ref=panel_in.at[sweep, h, dp],
            send_sem=panel_send.at[sweep, h],
            recv_sem=panel_recv.at[sweep, h],
            device_id=(target, cent),
            device_id_type=MESH,
        )

    def unit_scale(squares, sweep):
        mean = jnp.sum(squares, axis=1, keepdims=True) / D
        scale = jnp.where(sweep == 0, 1.0, lax.rsqrt(mean + EPSILON))
        return scale * lax.rsqrt(mean * scale * scale + EPSILON)

    def leave_origin(origin, carry):
        def step(i, inner):
            row_copy(origin, i).wait_send()
            return inner

        lax.fori_loop(0, LAYER - 1, step, 0)

        @pl.when(jnp.logical_and(origin <= z, z < N_Z - 1))
        def _():
            unit_copy(origin, 1).wait_send()

        @pl.when(jnp.logical_and(origin >= z, z > 0))
        def _():
            unit_copy(origin, 0).wait_send()

        @pl.when(origin != z)
        def _():
            rank_copy(origin).wait_send()

        return carry

    def sweep_step(sweep, carry):
        def unit_half(h):
            low_row, high_row = half * h, half * h + quarter
            top_squares = jnp.zeros((quarter, 128), F32)
            bottom_squares = jnp.zeros((quarter, 128), F32)
            for j in range(N_DP // 2):
                even = fresh[sweep, h, 2 * j].astype(F32)
                odd = fresh[sweep, h, 2 * j + 1].astype(F32)
                top = jnp.where(left, even, pltpu.roll(odd, 64, 1))
                bottom = jnp.where(left, pltpu.roll(even, 64, 1), odd)
                wide[:quarter, 128 * j : 128 * (j + 1)] = top
                wide[quarter:, 128 * j : 128 * (j + 1)] = bottom
                top_squares += top * top
                bottom_squares += bottom * bottom
            top_scale = unit_scale(top_squares, sweep)
            bottom_scale = unit_scale(bottom_squares, sweep)
            unit_cent[low_row:high_row] = (wide[:quarter] * top_scale).astype(BF16)
            unit_cent[high_row : half * (h + 1)] = (wide[quarter:] * bottom_scale).astype(BF16)

        def score(origin, start, size):
            mine = rows[pl.ds(origin * LAYER, LAYER)].reshape(LAYER * CAP, D)
            scores = lax.dot_general(
                unit_cent[start : start + size],
                mine,
                (((1,), (1,)), ((), ())),
                preferred_element_type=F32,
            )
            weights = jnp.exp(scores * (SHARPNESS / D))
            raw[start : start + size, lanes(origin * LAYER * CAP, LAYER * CAP)] = weights
            added = jnp.sum(weights, axis=0, keepdims=True)
            for j in range(N_X):
                piece = added[:, 128 * j : 128 * (j + 1)]
                if start > 0:
                    piece += part[sweep, j, pl.ds(origin, 1), :]
                part[sweep, j, pl.ds(origin, 1), :] = piece

        @pl.when(sweep == 0)
        def _():
            seen = fresh.at[0, :, pl.ds(0, 2 * (N_Y - 1))]
            pltpu.make_async_copy(seen, seen, first_sems.at[1]).wait()
            for h in range(2):
                unit_half(h)

            def score_arrived(g, inner):
                distance = (g + 1) // 2
                origin = z + jnp.where(lax.rem(g, 2) == 1, -distance, distance)

                @pl.when(jnp.logical_and(origin >= 0, origin < N_Z))
                def _():
                    def arrive(i, deep):
                        sender = seat_peer(i)
                        slot = rows.at[origin * LAYER + sender]
                        pltpu.make_async_copy(
                            slot, slot, x_recv.at[origin * LAYER + sender]
                        ).wait()
                        return deep

                    lax.fori_loop(0, LAYER - 1, arrive, 0)
                    score(origin, 0, BLOCK)

                return inner

            lax.fori_loop(0, 2 * N_Z - 1, score_arrived, 0)

        @pl.when(sweep > 0)
        def _():
            for h in range(2):
                seen = fresh.at[sweep, h, pl.ds(0, N_DP - 1)]
                pltpu.make_async_copy(seen, seen, fresh_recv.at[h]).wait()
                unit_half(h)

                def score_half(origin, inner):
                    score(origin, half * h, half)
                    return inner

                lax.fori_loop(0, N_Z, score_half, 0)

        exchange_seats(part, part_in, sweep, part_send, part_recv)
        parts = split(take_halves(part_in, sweep))
        by_row = jnp.zeros((LAYER, ROWS), F32)
        for layer in range(N_Z):
            product = jnp.dot(parts, picks[layer], preferred_element_type=F32)
            by_row += own_row(product, layer)
        line_in[sweep, z] = by_row[:N_Z]

        def send_line(i, inner):
            line_copy(sweep, i).start()
            return inner

        lax.fori_loop(1, N_Z, send_line, 0)
        seen = line_in.at[sweep, pl.ds(0, N_Z - 1)]
        pltpu.make_async_copy(seen, seen, line_recv.at[sweep]).wait()
        row_totals = line_in[sweep, 0]
        for layer in range(1, N_Z):
            row_totals += line_in[sweep, layer]
        parts = split(row_totals)
        by_slot = jnp.zeros((LAYER, LAYER * CAP), F32)
        for layer in range(N_Z):
            product = lax.dot_general(
                parts, picks[layer], (((1,), (1,)), ((), ())), preferred_element_type=F32
            )
            by_slot += own_row(product, layer)
        for j in range(N_X):
            total[sweep, j] = by_slot[:N_Z, 128 * j : 128 * (j + 1)]
        exchange_seats(total, total_in, sweep, total_send, total_recv)
        totals = take_halves(total_in, sweep)
        live = totals > 0.0
        inverse = jnp.where(live, 1.0 / jnp.where(live, totals, 1.0), 0.0)

        mass_part = jnp.zeros((BLOCK, 128), F32)
        for layer in range(N_Z):
            for j in range(N_X):
                start = layer * LAYER * CAP + 128 * j
                piece = slice(start, start + 128)
                shares = raw[:, piece] * inverse[layer : layer + 1, 128 * j : 128 * (j + 1)]
                low[:, piece] = shares.astype(BF16)
                mass_part += shares
        mass_row = jnp.sum(jnp.transpose(mass_part), axis=0, keepdims=True)
        for h in range(2):
            edge_out[h, 1:2, :] = mass_row[:, half * h : half * (h + 1)]

        def sum_step(i, inner):
            far_z = lax.rem(dp // N_Y + 1 - lax.rem(i, 2), 2)
            far_y = lax.rem(dp // 4 + 1 - i // 2, 2)
            j = far_z * 2 + far_y
            block_rows = rows[:, :, lanes(j * 256, 256)].reshape(SLOTS, 256)
            sums = jnp.dot(low[...], block_rows, preferred_element_type=F32)
            for h in range(2):
                for k in range(2):
                    top = sums[half * h : half * h + quarter, 128 * k : 128 * (k + 1)]
                    bottom = sums[half * h + quarter : half * (h + 1), 128 * k : 128 * (k + 1)]
                    even = jnp.where(left, top, pltpu.roll(bottom, 64, 1))
                    odd = jnp.where(left, pltpu.roll(top, 64, 1), bottom)
                    panel_out[sweep, h, 4 * j + 2 * k] = even.astype(BF16)
                    panel_out[sweep, h, 4 * j + 2 * k + 1] = odd.astype(BF16)
            for k in range(4):
                target = 4 * j + lax.rem(dp + 2 + k, 4)

                @pl.when(target != dp)
                def _():
                    panel_copy(sweep, 0, target).start()

            return inner

        lax.fori_loop(0, N_DP // 4, sum_step, 0)

        def send_second(i, inner):
            panel_copy(sweep, 1, dp_peer(i)).start()
            return inner

        lax.fori_loop(0, N_DP - 1, send_second, 0)

        for ref, sem, count in (
            (part_in, part_send, LAYER - 1),
            (line_in, line_send, N_Z - 1),
            (total_in, total_send, LAYER - 1),
        ):
            sent = ref.at[sweep, pl.ds(0, count)]
            pltpu.make_async_copy(sent, sent, sem.at[sweep]).wait()

        @pl.when(sweep == 0)
        def _():
            lax.fori_loop(0, N_Z, leave_origin, 0)

        for h in range(2):
            panel_in[sweep, h, dp] = panel_out[sweep, h, dp]
            seen = panel_in.at[sweep, h, pl.ds(0, N_DP - 1)]
            pltpu.make_async_copy(seen, seen, panel_recv.at[sweep, h]).wait()
            sums_panel = panel_in[sweep, h, 0].astype(F32)
            for j in range(1, N_DP):
                sums_panel += panel_in[sweep, h, j].astype(F32)

            @pl.when(sweep < ITERS - 1)
            def _():
                fresh[sweep + 1, h, dp] = sums_panel.astype(BF16)

                def send_fresh(i, inner):
                    fresh_copy(sweep + 1, h, i).start()
                    return inner

                lax.fori_loop(0, N_DP - 1, send_fresh, 0)

            @pl.when(sweep == ITERS - 1)
            def _():
                along = jnp.transpose(jnp.concatenate([sums_panel, sums_panel], axis=0))
                across = jnp.where(left, along[:PANEL], along[PANEL:])
                last_sums[h] = across
                edge_out[h, 0:1, :] = jnp.sum(across * across, axis=0, keepdims=True)

                def send_edge(i, inner):
                    edge_copy(h, i).start()
                    return inner

                lax.fori_loop(0, N_DP - 1, send_edge, 0)
                edge_in[h, dp] = edge_out[h]

        return carry

    lax.fori_loop(0, ITERS, sweep_step, 0)

    for h in range(2):
        seen = edge_in.at[h, pl.ds(0, N_DP - 1)]
        pltpu.make_async_copy(seen, seen, edge_recv.at[h]).wait()
        edges = edge_in[h, 0]
        for j in range(1, N_DP):
            edges += edge_in[h, j]
        scales = lax.rsqrt(edges[0:1] / D + EPSILON)
        out_ref[:, half * h : half * (h + 1)] = last_sums[h] * scales
        mass_ref[:, half * h : half * (h + 1)] = edges[1:2]

    for sweep in range(ITERS):
        for h in range(2):
            sent = panel_in.at[sweep, h, pl.ds(0, N_DP - 1)]
            pltpu.make_async_copy(sent, sent, panel_send.at[sweep, h]).wait()
    for h in range(2):
        sent = fresh.at[1, h, pl.ds(0, N_DP - 1)]
        pltpu.make_async_copy(sent, sent, fresh_send.at[h]).wait()
        sent = edge_in.at[h, pl.ds(0, N_DP - 1)]
        pltpu.make_async_copy(sent, sent, edge_send.at[h]).wait()
    pair_copy.wait_send()
    sent = fresh.at[0, :, pl.ds(0, 2 * (N_Y - 1))]
    pltpu.make_async_copy(sent, sent, first_sems.at[0]).wait()


def body(vectors, candidates, centroids):
    vmem = pl.BlockSpec(memory_space=pltpu.VMEM)
    dma = pltpu.SemaphoreType.DMA
    panel, mass = pl.pallas_call(
        kernel,
        out_shape=(
            jax.ShapeDtypeStruct((PANEL, BLOCK), F32),
            jax.ShapeDtypeStruct((1, BLOCK), F32),
        ),
        in_specs=[pl.BlockSpec(memory_space=pltpu.HBM)] * 3,
        out_specs=(vmem, vmem),
        scratch_shapes=[
            pltpu.VMEM((ROWS, D), BF16),
            pltpu.VMEM(candidates.shape[::-1], jnp.int32),
            pltpu.VMEM((PANEL, BLOCK), BF16),
            dma((3,)),
            pltpu.VMEM((N_Z, ROWS, D), BF16),
            pltpu.VMEM((N_Z, 2, LAYER, ROWS), jnp.int32),
            pltpu.VMEM((N_Z, LAYER * CAP, ROWS), BF16),
            pltpu.VMEM((N_Z, LAYER, CAP, D), BF16),
            pltpu.VMEM((N_CENT, CAP, D), BF16),
            pltpu.VMEM((BLOCK, SLOTS), F32),
            pltpu.VMEM((BLOCK, SLOTS), BF16),
            pltpu.VMEM((ITERS, N_X, N_Z, 128), F32),
            pltpu.VMEM((ITERS, LAYER, N_Z, 128), F32),
            pltpu.VMEM((ITERS, N_Z, N_Z, ROWS), F32),
            pltpu.VMEM((ITERS, N_X, N_Z, 128), F32),
            pltpu.VMEM((ITERS, LAYER, N_Z, 128), F32),
            pltpu.VMEM((BLOCK // 2, D), F32),
            pltpu.VMEM((BLOCK, D), BF16),
            pltpu.VMEM((ITERS, 2, N_DP, BLOCK // 4, 128), BF16),
            pltpu.VMEM((ITERS, 2, N_DP, BLOCK // 4, 128), BF16),
            pltpu.VMEM((ITERS, 2, N_DP, BLOCK // 4, 128), BF16),
            pltpu.VMEM((2, PANEL, 128), F32),
            pltpu.VMEM((2, 2, 128), F32),
            pltpu.VMEM((2, N_DP, 2, 128), F32),
            pltpu.SemaphoreType.REGULAR,
            dma((N_Z, 2)),
            dma((N_Z,)),
            dma((N_Z,)),
            dma((N_Z,)),
            dma((N_Z, LAYER)),
            dma((N_CENT,)),
            dma((2,)),
            dma((2,)),
            dma((ITERS,)),
            dma((ITERS,)),
            dma((ITERS,)),
            dma((ITERS,)),
            dma((ITERS,)),
            dma((ITERS,)),
            dma((ITERS, 2)),
            dma((ITERS, 2)),
            dma((2,)),
            dma((2,)),
            dma((2,)),
            dma((2,)),
        ],
        compiler_params=pltpu.CompilerParams(
            collective_id=0, has_side_effects=True, vmem_limit_bytes=60 * 1024 * 1024
        ),
        cost_estimate=pl.CostEstimate(
            flops=9 * 2 * SLOTS * BLOCK * D // 2, bytes_accessed=4 << 20, transcendentals=SLOTS * BLOCK
        ),
        name="soft_kmeans",
    )(vectors, candidates.T, centroids.T)
    return panel.T, mass.reshape(BLOCK)


def solution(mesh):
    return jax.shard_map(
        body,
        mesh=mesh,
        in_specs=(P(("dp", "cent"), None), P(("dp", "cent"), None), P("cent", "dp")),
        out_specs=(P("cent", "dp"), P("cent")),
        check_vma=False,
    )
```

```python
import functools

import jax
import jax.numpy as jnp
from jax import lax
from jax.experimental import pallas as pl
from jax.experimental.pallas import tpu as pltpu
from jax.sharding import PartitionSpec as P

ITERS = 2
EPSILON = 1e-06
SHARPNESS = 20.0

D = 1024
ROWS = 256
BLOCK = 256
CAP = 64
N_DP = 16
N_CENT = 32
EARLY = 4
N_X = 4
N_Y = 8
N_Z = 4
LAYER = 8
SLOTS = N_CENT * CAP
PANEL = D // N_DP

F32 = jnp.float32
BF16 = jnp.bfloat16
MESH = pl.DeviceIdType.MESH


def lanes(start, size):
    return pl.ds(pl.multiple_of(start, 128), size)


def kernel(
    vec_hbm,
    cand_hbm,
    cent_hbm,
    out_ref,
    mass_ref,
    vec_ref,
    cand_ref,
    cent_ref,
    fetch_sems,
    units,
    ranks,
    picks,
    packed,
    rows,
    raw,
    low,
    part,
    part_in,
    line_in,
    total,
    total_in,
    wide,
    unit_cent,
    panel_out,
    panel_in,
    fresh,
    last_sums,
    edge_out,
    edge_in,
    vouched,
    z_send,
    z_recv,
    rank_send,
    rank_recv,
    x_send,
    x_recv,
    pair_sems,
    first_sems,
    part_send,
    part_recv,
    line_send,
    line_recv,
    total_send,
    total_recv,
    panel_send,
    panel_recv,
    fresh_send,
    fresh_recv,
    edge_send,
    edge_recv,
):
    dp = lax.axis_index("dp")
    cent = lax.axis_index("cent")
    x = cent // LAYER
    z = (cent // 2) % N_Z
    core = cent % 2
    seat = x * 2 + core

    def offset(i):
        return 4 + i // 2 - lax.rem(i, 2) * (2 * (i // 2) + 1)

    def dp_peer(i):
        z_of = lax.rem(dp // N_Y + 1 - lax.rem(i, 2), 2)
        return z_of * N_Y + lax.rem(dp + offset(i // 2), N_Y)

    def y_peer(i):
        return (dp // N_Y) * N_Y + lax.rem(dp + offset(i), N_Y)

    other_dp = lax.rem(dp + N_Y, N_DP)

    def seat_peer(i):
        return lax.rem(seat + offset(i), LAYER)

    def z_peer(i):
        return lax.rem(z + i, N_Z)

    def at_seat(other):
        return (dp, (other // 2) * LAYER + z * 2 + other % 2)

    def at_layer(other):
        return (dp, x * LAYER + other * 2 + core)

    barrier = pltpu.get_barrier_semaphore()

    def greet_seat(i, carry):
        pl.semaphore_signal(barrier, inc=1, device_id=at_seat(seat_peer(i)), device_id_type=MESH)
        return carry

    def greet_layer(i, carry):
        pl.semaphore_signal(barrier, inc=1, device_id=at_layer(z_peer(i)), device_id_type=MESH)
        return carry

    def greet_y(i, carry):
        pl.semaphore_signal(barrier, inc=1, device_id=(y_peer(i), cent), device_id_type=MESH)
        return carry

    lax.fori_loop(0, LAYER - 1, greet_seat, 0)
    lax.fori_loop(1, N_Z, greet_layer, 0)
    lax.fori_loop(0, N_Y - 1, greet_y, 0)
    pl.semaphore_signal(barrier, inc=1, device_id=(other_dp, cent), device_id_type=MESH)

    fetches = [
        pltpu.make_async_copy(source, place, sem)
        for source, place, sem in (
            (vec_hbm, vec_ref, fetch_sems.at[0]),
            (cand_hbm, cand_ref, fetch_sems.at[1]),
            (cent_hbm, cent_ref, fetch_sems.at[2]),
        )
    ]
    for fetch in fetches:
        fetch.start()

    fetches[0].wait()
    vec = vec_ref[...].astype(F32)
    vec_scale = lax.rsqrt(jnp.mean(vec * vec, axis=1, keepdims=True) + EPSILON)
    units[z] = (vec * vec_scale).astype(BF16)

    pl.semaphore_wait(barrier, LAYER - 1 + N_Z - 1 + N_Y)
    pl.semaphore_signal(vouched, inc=1, device_id=(other_dp, cent), device_id_type=MESH)

    def unit_copy(origin, side):
        return pltpu.make_async_remote_copy(
            src_ref=units.at[origin],
            dst_ref=units.at[origin],
            send_sem=z_send.at[origin, side],
            recv_sem=z_recv.at[origin],
            device_id=at_layer(z + 2 * side - 1),
            device_id_type=MESH,
        )

    def start_up(origin):
        @pl.when(z < N_Z - 1)
        def _():
            unit_copy(origin, 1).start()

    def start_down(origin):
        @pl.when(z > 0)
        def _():
            unit_copy(origin, 0).start()

    @pl.when(core == 0)
    def _():
        start_up(z)
        start_down(z)

    fetches[1].wait()
    cand = cand_ref[...]
    place = lax.broadcasted_iota(jnp.int32, (N_CENT, ROWS), 0)
    block = ((place >> 1) & (N_X - 1)) * LAYER + (place >> 3) * 2 + (place & 1)
    named = cand[0:1, :] == block
    for j in range(1, cand.shape[0]):
        named = jnp.logical_or(named, cand[j : j + 1, :] == block)
    named_f = jnp.where(named, 1.0, 0.0)
    first = lax.broadcasted_iota(jnp.int32, (ROWS, ROWS), 0)
    second = lax.broadcasted_iota(jnp.int32, (ROWS, ROWS), 1)
    before = jnp.where(first < second, 1.0, 0.0).astype(BF16)
    rank = jnp.dot(named_f.astype(BF16), before, preferred_element_type=F32)
    slots = jnp.where(named, rank, -1.0).astype(jnp.int32)
    for layer in range(N_Z):
        ranks[layer, 0] = slots[layer * LAYER : (layer + 1) * LAYER]

    slot_iota = lax.broadcasted_iota(jnp.int32, (CAP, ROWS), 0)

    def pick_rows(rank_rows):
        picks = [
            jnp.where(rank_rows[j : j + 1, :] == slot_iota, 1.0, 0.0).astype(BF16)
            for j in range(LAYER)
        ]
        return jnp.concatenate(picks, axis=0)

    def pack(origin, rank_rows):
        picks[origin] = pick_rows(rank_rows)
        chosen = jnp.dot(picks[origin], units[origin], preferred_element_type=F32)
        packed[origin] = chosen.astype(BF16).reshape(LAYER, CAP, D)
        rows[origin * LAYER + seat] = packed[origin, seat]

    pack(z, ranks[z, 0])

    def rank_copy(layer):
        return pltpu.make_async_remote_copy(
            src_ref=ranks.at[layer, 0],
            dst_ref=ranks.at[z, 1],
            send_sem=rank_send.at[layer],
            recv_sem=rank_recv.at[z],
            device_id=at_layer(layer),
            device_id_type=MESH,
        )

    def send_rank(i, carry):
        rank_copy(z_peer(i)).start()
        return carry

    lax.fori_loop(1, N_Z, send_rank, 0)

    def first_copy(which, i):
        return pltpu.make_async_remote_copy(
            src_ref=fresh.at[0, :, which],
            dst_ref=fresh.at[0, :, which],
            send_sem=first_sems.at[0],
            recv_sem=first_sems.at[1],
            device_id=(y_peer(i), cent),
            device_id_type=MESH,
        )

    def fresh_copy(sweep, h, i):
        return pltpu.make_async_remote_copy(
            src_ref=fresh.at[sweep, h, dp],
            dst_ref=fresh.at[sweep, h, dp],
            send_sem=fresh_send.at[h],
            recv_sem=fresh_recv.at[h],
            device_id=(dp_peer(i), cent),
            device_id_type=MESH,
        )

    def row_copy(origin, i):
        target = seat_peer(i)
        return pltpu.make_async_remote_copy(
            src_ref=packed.at[origin, target],
            dst_ref=rows.at[origin * LAYER + seat],
            send_sem=x_send.at[origin, target],
            recv_sem=x_recv.at[origin * LAYER + seat],
            device_id=at_seat(target),
            device_id_type=MESH,
        )

    def send_packed(origin):
        def step(i, carry):
            row_copy(origin, i).start()
            return carry

        lax.fori_loop(0, LAYER - 1, step, 0)

    send_packed(z)

    @pl.when(core == 1)
    def _():
        for i in range(EARLY):
            row_copy(z, i).wait_send()
        start_up(z)
        start_down(z)

    fetches[2].wait()
    half = BLOCK // 2
    quarter = half // 2
    left = lax.broadcasted_iota(jnp.int32, (quarter, 128), 1) < PANEL
    for h in range(2):
        across = cent_ref[:, half * h : half * (h + 1)].astype(F32)
        along = jnp.transpose(jnp.concatenate([across, across], axis=0))
        fresh[0, h, dp] = jnp.where(left, along[:quarter], along[quarter:]).astype(BF16)

    pair_copy = pltpu.make_async_remote_copy(
        src_ref=fresh.at[0, :, dp],
        dst_ref=fresh.at[0, :, dp],
        send_sem=pair_sems.at[0],
        recv_sem=pair_sems.at[1],
        device_id=(other_dp, cent),
        device_id_type=MESH,
    )
    pair_copy.start()

    def event(e, carry):
        distance = (e + 1) // 2
        up = lax.rem(e, 2)
        origin = z + jnp.where(up == 1, -distance, distance)

        @pl.when(jnp.logical_and(origin >= 0, origin < N_Z))
        def _():
            unit_copy(origin, 0).wait_recv()

            @pl.when(up == 1)
            def _():
                start_up(origin)

            @pl.when(up == 0)
            def _():
                start_down(origin)

            rank_copy_in(origin).wait_recv()

        return carry

    def pack_event(e, carry):
        distance = (e + 1) // 2
        up = lax.rem(e, 2)
        origin = z + jnp.where(up == 1, -distance, distance)

        @pl.when(jnp.logical_and(origin >= 0, origin < N_Z))
        def _():
            pack(origin, ranks[origin, 1])
            send_packed(origin)

        return carry

    def rank_copy_in(origin):
        return pltpu.make_async_remote_copy(
            src_ref=ranks.at[origin, 0],
            dst_ref=ranks.at[origin, 1],
            send_sem=rank_send.at[origin],
            recv_sem=rank_recv.at[origin],
            device_id=at_layer(origin),
            device_id_type=MESH,
        )

    lax.fori_loop(1, 3, event, 0)
    lax.fori_loop(1, 3, pack_event, 0)
    pair_copy.wait_recv()

    def send_first(i, carry):
        first_copy(dp, i).start()
        first_copy(other_dp, i).start()
        return carry

    lax.fori_loop(0, N_Y - 1, send_first, 0)
    lax.fori_loop(3, 5, event, 0)
    lax.fori_loop(3, 5, pack_event, 0)
    lax.fori_loop(5, 7, event, 0)
    lax.fori_loop(5, 7, pack_event, 0)
    pl.semaphore_wait(vouched, 1)

    left_four = lax.broadcasted_iota(jnp.int32, (N_Z, 128), 1) < CAP
    layer_iota = lax.broadcasted_iota(jnp.int32, (LAYER, 1), 0)

    def take_halves(ref, sweep):
        pieces = []
        for j in range(LAYER // 2):
            even = ref[sweep, 2 * j]
            odd = ref[sweep, 2 * j + 1]
            first_core = jnp.where(left_four, even, pltpu.roll(odd, 64, 1))
            second_core = jnp.where(left_four, pltpu.roll(even, 64, 1), odd)
            pieces.append(jnp.where(core == 0, first_core, second_core))
        return jnp.concatenate(pieces, axis=1)

    def split(four):
        zeros = jnp.zeros((LAYER - N_Z, four.shape[1]), F32)
        value = jnp.concatenate([four, zeros], axis=0)
        high = value.astype(BF16).astype(F32)
        rest = value - high
        middle = rest.astype(BF16).astype(F32)
        return jnp.concatenate([high, middle, rest - middle], axis=0).astype(BF16)

    def own_row(product, layer):
        added = product[:LAYER] + product[LAYER : 2 * LAYER] + product[2 * LAYER :]
        return jnp.where(layer_iota == layer, added, 0.0)

    def seat_copy(source, target, sweep, i, send_sem, recv_sem):
        other = seat_peer(i)
        return pltpu.make_async_remote_copy(
            src_ref=source.at[sweep, other // 2],
            dst_ref=target.at[sweep, seat],
            send_sem=send_sem.at[sweep],
            recv_sem=recv_sem.at[sweep],
            device_id=at_seat(other),
            device_id_type=MESH,
        )

    def exchange_seats(source, target, sweep, send_sem, recv_sem):
        def step(i, carry):
            seat_copy(source, target, sweep, i, send_sem, recv_sem).start()
            return carry

        lax.fori_loop(0, LAYER - 1, step, 0)
        target[sweep, seat] = source[sweep, x]
        seen = target.at[sweep, pl.ds(0, LAYER - 1)]
        pltpu.make_async_copy(seen, seen, recv_sem.at[sweep]).wait()

    def line_copy(sweep, i):
        return pltpu.make_async_remote_copy(
            src_ref=line_in.at[sweep, z],
            dst_ref=line_in.at[sweep, z],
            send_sem=line_send.at[sweep],
            recv_sem=line_recv.at[sweep],
            device_id=at_layer(z_peer(i)),
            device_id_type=MESH,
        )

    def edge_copy(h, i):
        return pltpu.make_async_remote_copy(
            src_ref=edge_out.at[h],
            dst_ref=edge_in.at[h, dp],
            send_sem=edge_send.at[h],
            recv_sem=edge_recv.at[h],
            device_id=(dp_peer(i), cent),
            device_id_type=MESH,
        )

    def panel_copy(sweep, h, target):
        return pltpu.make_async_remote_copy(
            src_ref=panel_out.at[sweep, h, target],
            dst_ref=panel_in.at[sweep, h, dp],
            send_sem=panel_send.at[sweep, h],
            recv_sem=panel_recv.at[sweep, h],
            device_id=(target, cent),
            device_id_type=MESH,
        )

    def unit_scale(squares, sweep):
        mean = jnp.sum(squares, axis=1, keepdims=True) / D
        scale = jnp.where(sweep == 0, 1.0, lax.rsqrt(mean + EPSILON))
        return scale * lax.rsqrt(mean * scale * scale + EPSILON)

    def leave_origin(origin, carry):
        def step(i, inner):
            @pl.when(jnp.logical_or(i >= EARLY, jnp.logical_or(origin != z, core == 0)))
            def _():
                row_copy(origin, i).wait_send()

            return inner

        lax.fori_loop(0, LAYER - 1, step, 0)

        @pl.when(jnp.logical_and(origin <= z, z < N_Z - 1))
        def _():
            unit_copy(origin, 1).wait_send()

        @pl.when(jnp.logical_and(origin >= z, z > 0))
        def _():
            unit_copy(origin, 0).wait_send()

        @pl.when(origin != z)
        def _():
            rank_copy(origin).wait_send()

        return carry

    def sweep_step(sweep, carry):
        def unit_half(h):
            low_row, high_row = half * h, half * h + quarter
            top_squares = jnp.zeros((quarter, 128), F32)
            bottom_squares = jnp.zeros((quarter, 128), F32)
            for j in range(N_DP // 2):
                even = fresh[sweep, h, 2 * j].astype(F32)
                odd = fresh[sweep, h, 2 * j + 1].astype(F32)
                top = jnp.where(left, even, pltpu.roll(odd, 64, 1))
                bottom = jnp.where(left, pltpu.roll(even, 64, 1), odd)
                wide[:quarter, 128 * j : 128 * (j + 1)] = top
                wide[quarter:, 128 * j : 128 * (j + 1)] = bottom
                top_squares += top * top
                bottom_squares += bottom * bottom
            top_scale = unit_scale(top_squares, sweep)
            bottom_scale = unit_scale(bottom_squares, sweep)
            unit_cent[low_row:high_row] = (wide[:quarter] * top_scale).astype(BF16)
            unit_cent[high_row : half * (h + 1)] = (wide[quarter:] * bottom_scale).astype(BF16)

        def score(origin, start, size):
            mine = rows[pl.ds(origin * LAYER, LAYER)].reshape(LAYER * CAP, D)
            scores = lax.dot_general(
                unit_cent[start : start + size],
                mine,
                (((1,), (1,)), ((), ())),
                preferred_element_type=F32,
            )
            weights = jnp.exp(scores * (SHARPNESS / D))
            raw[start : start + size, lanes(origin * LAYER * CAP, LAYER * CAP)] = weights
            added = jnp.sum(weights, axis=0, keepdims=True)
            for j in range(N_X):
                piece = added[:, 128 * j : 128 * (j + 1)]
                if start > 0:
                    piece += part[sweep, j, pl.ds(origin, 1), :]
                part[sweep, j, pl.ds(origin, 1), :] = piece

        @pl.when(sweep == 0)
        def _():
            seen = fresh.at[0, :, pl.ds(0, 2 * (N_Y - 1))]
            pltpu.make_async_copy(seen, seen, first_sems.at[1]).wait()
            for h in range(2):
                unit_half(h)

            def score_arrived(g, inner):
                distance = (g + 1) // 2
                origin = z + jnp.where(lax.rem(g, 2) == 1, -distance, distance)

                @pl.when(jnp.logical_and(origin >= 0, origin < N_Z))
                def _():
                    def arrive(i, deep):
                        sender = seat_peer(i)
                        slot = rows.at[origin * LAYER + sender]
                        pltpu.make_async_copy(
                            slot, slot, x_recv.at[origin * LAYER + sender]
                        ).wait()
                        return deep

                    lax.fori_loop(0, LAYER - 1, arrive, 0)
                    score(origin, 0, BLOCK)

                return inner

            lax.fori_loop(0, 2 * N_Z - 1, score_arrived, 0)

        @pl.when(sweep > 0)
        def _():
            for h in range(2):
                seen = fresh.at[sweep, h, pl.ds(0, N_DP - 1)]
                pltpu.make_async_copy(seen, seen, fresh_recv.at[h]).wait()
                unit_half(h)

                def score_half(origin, inner):
                    score(origin, half * h, half)
                    return inner

                lax.fori_loop(0, N_Z, score_half, 0)

        exchange_seats(part, part_in, sweep, part_send, part_recv)
        parts = split(take_halves(part_in, sweep))
        by_row = jnp.zeros((LAYER, ROWS), F32)
        for layer in range(N_Z):
            product = jnp.dot(parts, picks[layer], preferred_element_type=F32)
            by_row += own_row(product, layer)
        line_in[sweep, z] = by_row[:N_Z]

        def send_line(i, inner):
            line_copy(sweep, i).start()
            return inner

        lax.fori_loop(1, N_Z, send_line, 0)
        seen = line_in.at[sweep, pl.ds(0, N_Z - 1)]
        pltpu.make_async_copy(seen, seen, line_recv.at[sweep]).wait()
        row_totals = line_in[sweep, 0]
        for layer in range(1, N_Z):
            row_totals += line_in[sweep, layer]
        parts = split(row_totals)
        by_slot = jnp.zeros((LAYER, LAYER * CAP), F32)
        for layer in range(N_Z):
            product = lax.dot_general(
                parts, picks[layer], (((1,), (1,)), ((), ())), preferred_element_type=F32
            )
            by_slot += own_row(product, layer)
        for j in range(N_X):
            total[sweep, j] = by_slot[:N_Z, 128 * j : 128 * (j + 1)]
        exchange_seats(total, total_in, sweep, total_send, total_recv)
        totals = take_halves(total_in, sweep)
        live = totals > 0.0
        inverse = jnp.where(live, 1.0 / jnp.where(live, totals, 1.0), 0.0)

        mass_part = jnp.zeros((BLOCK, 128), F32)
        for layer in range(N_Z):
            for j in range(N_X):
                start = layer * LAYER * CAP + 128 * j
                piece = slice(start, start + 128)
                shares = raw[:, piece] * inverse[layer : layer + 1, 128 * j : 128 * (j + 1)]
                low[:, piece] = shares.astype(BF16)
                mass_part += shares
        mass_row = jnp.sum(jnp.transpose(mass_part), axis=0, keepdims=True)
        for h in range(2):
            edge_out[h, 1:2, :] = mass_row[:, half * h : half * (h + 1)]

        def sum_step(i, inner):
            far_z = lax.rem(dp // N_Y + 1 - lax.rem(i, 2), 2)
            far_y = lax.rem(dp // 4 + 1 - i // 2, 2)
            j = far_z * 2 + far_y
            block_rows = rows[:, :, lanes(j * 256, 256)].reshape(SLOTS, 256)
            sums = jnp.dot(low[...], block_rows, preferred_element_type=F32)
            for h in range(2):
                for k in range(2):
                    top = sums[half * h : half * h + quarter, 128 * k : 128 * (k + 1)]
                    bottom = sums[half * h + quarter : half * (h + 1), 128 * k : 128 * (k + 1)]
                    even = jnp.where(left, top, pltpu.roll(bottom, 64, 1))
                    odd = jnp.where(left, pltpu.roll(top, 64, 1), bottom)
                    panel_out[sweep, h, 4 * j + 2 * k] = even.astype(BF16)
                    panel_out[sweep, h, 4 * j + 2 * k + 1] = odd.astype(BF16)
            for k in range(4):
                target = 4 * j + lax.rem(dp + 2 + k, 4)

                @pl.when(target != dp)
                def _():
                    panel_copy(sweep, 0, target).start()

            return inner

        lax.fori_loop(0, N_DP // 4, sum_step, 0)

        def send_second(i, inner):
            panel_copy(sweep, 1, dp_peer(i)).start()
            return inner

        lax.fori_loop(0, N_DP - 1, send_second, 0)

        for ref, sem, count in (
            (part_in, part_send, LAYER - 1),
            (line_in, line_send, N_Z - 1),
            (total_in, total_send, LAYER - 1),
        ):
            sent = ref.at[sweep, pl.ds(0, count)]
            pltpu.make_async_copy(sent, sent, sem.at[sweep]).wait()

        @pl.when(sweep == 0)
        def _():
            lax.fori_loop(0, N_Z, leave_origin, 0)

        for h in range(2):
            panel_in[sweep, h, dp] = panel_out[sweep, h, dp]
            seen = panel_in.at[sweep, h, pl.ds(0, N_DP - 1)]
            pltpu.make_async_copy(seen, seen, panel_recv.at[sweep, h]).wait()
            sums_panel = panel_in[sweep, h, 0].astype(F32)
            for j in range(1, N_DP):
                sums_panel += panel_in[sweep, h, j].astype(F32)

            @pl.when(sweep < ITERS - 1)
            def _():
                fresh[sweep + 1, h, dp] = sums_panel.astype(BF16)

                def send_fresh(i, inner):
                    fresh_copy(sweep + 1, h, i).start()
                    return inner

                lax.fori_loop(0, N_DP - 1, send_fresh, 0)

            @pl.when(sweep == ITERS - 1)
            def _():
                along = jnp.transpose(jnp.concatenate([sums_panel, sums_panel], axis=0))
                across = jnp.where(left, along[:PANEL], along[PANEL:])
                last_sums[h] = across
                edge_out[h, 0:1, :] = jnp.sum(across * across, axis=0, keepdims=True)

                def send_edge(i, inner):
                    edge_copy(h, i).start()
                    return inner

                lax.fori_loop(0, N_DP - 1, send_edge, 0)
                edge_in[h, dp] = edge_out[h]

        return carry

    lax.fori_loop(0, ITERS, sweep_step, 0)

    for h in range(2):
        seen = edge_in.at[h, pl.ds(0, N_DP - 1)]
        pltpu.make_async_copy(seen, seen, edge_recv.at[h]).wait()
        edges = edge_in[h, 0]
        for j in range(1, N_DP):
            edges += edge_in[h, j]
        scales = lax.rsqrt(edges[0:1] / D + EPSILON)
        out_ref[:, half * h : half * (h + 1)] = last_sums[h] * scales
        mass_ref[:, half * h : half * (h + 1)] = edges[1:2]

    for sweep in range(ITERS):
        for h in range(2):
            sent = panel_in.at[sweep, h, pl.ds(0, N_DP - 1)]
            pltpu.make_async_copy(sent, sent, panel_send.at[sweep, h]).wait()
    for h in range(2):
        sent = fresh.at[1, h, pl.ds(0, N_DP - 1)]
        pltpu.make_async_copy(sent, sent, fresh_send.at[h]).wait()
        sent = edge_in.at[h, pl.ds(0, N_DP - 1)]
        pltpu.make_async_copy(sent, sent, edge_send.at[h]).wait()
    pair_copy.wait_send()
    sent = fresh.at[0, :, pl.ds(0, 2 * (N_Y - 1))]
    pltpu.make_async_copy(sent, sent, first_sems.at[0]).wait()


def body(vectors, candidates, centroids):
    vmem = pl.BlockSpec(memory_space=pltpu.VMEM)
    dma = pltpu.SemaphoreType.DMA
    panel, mass = pl.pallas_call(
        kernel,
        out_shape=(
            jax.ShapeDtypeStruct((PANEL, BLOCK), F32),
            jax.ShapeDtypeStruct((1, BLOCK), F32),
        ),
        in_specs=[pl.BlockSpec(memory_space=pltpu.HBM)] * 3,
        out_specs=(vmem, vmem),
        scratch_shapes=[
            pltpu.VMEM((ROWS, D), BF16),
            pltpu.VMEM(candidates.shape[::-1], jnp.int32),
            pltpu.VMEM((PANEL, BLOCK), BF16),
            dma((3,)),
            pltpu.VMEM((N_Z, ROWS, D), BF16),
            pltpu.VMEM((N_Z, 2, LAYER, ROWS), jnp.int32),
            pltpu.VMEM((N_Z, LAYER * CAP, ROWS), BF16),
            pltpu.VMEM((N_Z, LAYER, CAP, D), BF16),
            pltpu.VMEM((N_CENT, CAP, D), BF16),
            pltpu.VMEM((BLOCK, SLOTS), F32),
            pltpu.VMEM((BLOCK, SLOTS), BF16),
            pltpu.VMEM((ITERS, N_X, N_Z, 128), F32),
            pltpu.VMEM((ITERS, LAYER, N_Z, 128), F32),
            pltpu.VMEM((ITERS, N_Z, N_Z, ROWS), F32),
            pltpu.VMEM((ITERS, N_X, N_Z, 128), F32),
            pltpu.VMEM((ITERS, LAYER, N_Z, 128), F32),
            pltpu.VMEM((BLOCK // 2, D), F32),
            pltpu.VMEM((BLOCK, D), BF16),
            pltpu.VMEM((ITERS, 2, N_DP, BLOCK // 4, 128), BF16),
            pltpu.VMEM((ITERS, 2, N_DP, BLOCK // 4, 128), BF16),
            pltpu.VMEM((ITERS, 2, N_DP, BLOCK // 4, 128), BF16),
            pltpu.VMEM((2, PANEL, 128), F32),
            pltpu.VMEM((2, 2, 128), F32),
            pltpu.VMEM((2, N_DP, 2, 128), F32),
            pltpu.SemaphoreType.REGULAR,
            dma((N_Z, 2)),
            dma((N_Z,)),
            dma((N_Z,)),
            dma((N_Z,)),
            dma((N_Z, LAYER)),
            dma((N_CENT,)),
            dma((2,)),
            dma((2,)),
            dma((ITERS,)),
            dma((ITERS,)),
            dma((ITERS,)),
            dma((ITERS,)),
            dma((ITERS,)),
            dma((ITERS,)),
            dma((ITERS, 2)),
            dma((ITERS, 2)),
            dma((2,)),
            dma((2,)),
            dma((2,)),
            dma((2,)),
        ],
        compiler_params=pltpu.CompilerParams(
            collective_id=0, has_side_effects=True, vmem_limit_bytes=60 * 1024 * 1024
        ),
        cost_estimate=pl.CostEstimate(
            flops=9 * 2 * SLOTS * BLOCK * D // 2, bytes_accessed=4 << 20, transcendentals=SLOTS * BLOCK
        ),
        name="soft_kmeans",
    )(vectors, candidates.T, centroids.T)
    return panel.T, mass.reshape(BLOCK)


def solution(mesh):
    return jax.shard_map(
        body,
        mesh=mesh,
        in_specs=(P(("dp", "cent"), None), P(("dp", "cent"), None), P("cent", "dp")),
        out_specs=(P("cent", "dp"), P("cent")),
        check_vma=False,
    )
```
